32 devices in a mesh: blk: 8 (over y, x, core), mpo: 4 (over z).
Axes of the slice: x: 2, y: 2, z: 4, core: 2. Of those that a mesh axis runs over, the one named last changes fastest.
Arguments:
- theta: float32 [16, 128, 16, 128], P('blk'), may hold values from -6 to 6
- block_dims: int32 [16, 2], P('blk'), may hold values from 32 to 128, as said below
- pair_mask: int32 [24, 16], P(None, 'blk'), may hold values 0 or 1
- term_charge: int32 [24], replicated, may hold values from -1 to 1
- left_env: float32 [24, 16, 128, 128], P('mpo', 'blk'), may hold values from -0.5 to 0.5
- right_env: float32 [24, 16, 128, 128], P('mpo', 'blk'), may hold values from -0.5 to 0.5
- site_one: float32 [24, 4, 4], replicated, may hold values from -0.625 to 0.625
- site_two: float32 [24, 4, 4], replicated, may hold values from -3 to 3
Outputs:
- hpsi: float32 [16, 128, 16, 128], P('blk', 'mpo')
The draws below stay inside these ranges and needn't reach their ends.
Inputs may be any that keep to these rules, and one draw needn't show every extreme that they name: `block_dims`: kept dimensions of each sector; rows and columns of a block beyond them are empty. The first sector keeps 128 on both sides.
All inputs are finite; a program needn't handle non-finite values. No bound on the sum of `pair_mask` on one device may be relied on, other than what follows from the above.
Results may differ from the reference program's by a relative error of at most 0.0003.
Values sent between devices are 32-bit elements; how exact they have to be, the bound alone decides.
No kernel may reach another device: no remote copies, remote signals or barrier semaphores. Data moves between devices by JAX's collectives and lax.ppermute only.
A program may use at most 64 MiB of HBM per device.

```python
import jax
import jax.numpy as jnp
from jax import lax

BOND_CAP = 128
SITE = 4
NSEC = 16
NTERM = 24


def draw_block_dims(key, part):
    values = jax.random.randint(key, (NSEC, 2), BOND_CAP // 4, BOND_CAP + 1)
    leading = jnp.arange(NSEC)[:, None] == 0
    return jnp.where(leading, BOND_CAP, values).astype(jnp.int32)


def with_ends(values, own_key, least, high):
    longest = values.shape.index(max(values.shape))
    spots = []
    for shift in (0, 1):
        where = [jax.random.randint(jax.random.fold_in(own_key, axis), (), 0, length) for axis, length in enumerate(values.shape)]
        where[longest] = (where[longest] + shift) % values.shape[longest]
        spots.append(tuple(where))
    return values.at[spots[0]].set(least).at[spots[1]].set(high)


def shard_levels(stream_key, shape, split, low, largest):
    def one(position, blocks):
        heights = jax.random.uniform(jax.random.fold_in(jax.random.fold_in(stream_key, 6), position), (blocks,), jnp.float32, low / len(split), largest / len(split))
        return jnp.repeat(jnp.exp(heights), shape[position] // blocks).reshape((-1,) + (1,) * (len(shape) - position - 1))

    gain = one(*split[0])
    for cut in split[1:]:
        gain = gain * one(*cut)
    return gain


def scatter_about(key, extent, spread, bound, cuts=(), kind=jnp.bfloat16):
    array = spread * jax.random.normal(key, extent, jnp.float32)
    if cuts:
        array = array * shard_levels(key, extent, cuts, -0.22, 0.18)
    return jnp.clip(array, -bound, bound).astype(kind)


def setup_inputs(seed: int = 0) -> dict:
    streams_of = jax.random.split(jax.random.key(seed), 9)
    return {
        "theta": scatter_about(streams_of[0], (NSEC, BOND_CAP, SITE * SITE, BOND_CAP), 1.0, 6.0, ((0, 8),), jnp.float32),
        "block_dims": draw_block_dims(jax.random.fold_in(streams_of[8], 71), 0),
        "pair_mask": with_ends((jax.random.randint(streams_of[2], (NTERM, NSEC), 0, 4) < 3).astype(jnp.int32), jax.random.fold_in(streams_of[2], 1), 0, 1),
        "term_charge": with_ends(jax.random.randint(streams_of[3], (NTERM,), -1, 2), jax.random.fold_in(streams_of[3], 1), -1, 1).astype(jnp.int32),
        "left_env": scatter_about(streams_of[4], (NTERM, NSEC, BOND_CAP, BOND_CAP), BOND_CAP ** -0.5, 0.5, ((0, 4), (1, 8)), jnp.float32),
        "right_env": scatter_about(streams_of[5], (NTERM, NSEC, BOND_CAP, BOND_CAP), BOND_CAP ** -0.5, 0.5, ((0, 4), (1, 8)), jnp.float32),
        "site_one": scatter_about(streams_of[6], (NTERM, SITE, SITE), (SITE * NTERM) ** -0.5, 0.625, (), jnp.float32),
        "site_two": scatter_about(streams_of[7], (NTERM, SITE, SITE), SITE ** -0.5, 3.0, (), jnp.float32),
    }


def sector_mask(block_dims, bond_cap):
    positions = jnp.arange(bond_cap, dtype=jnp.int32)
    left_ok = positions[None, :] < block_dims[:, 0:1]
    right_ok = positions[None, :] < block_dims[:, 1:2]
    return (left_ok[:, :, None] & right_ok[:, None, :]).astype(jnp.float32)


def reference(theta, block_dims, pair_mask, term_charge, left_env, right_env, site_one, site_two):
    block_mask = sector_mask(block_dims, BOND_CAP)
    masked = theta * block_mask[:, :, None, :]
    padded = jnp.pad(masked, ((1, 1), (0, 0), (0, 0), (0, 0)))
    highest = lax.Precision.HIGHEST

    def step(summed, items):
        left_block, right_block, first_op, second_op, charge, allowed = items
        start = (1 - charge).astype(jnp.int32)
        source = lax.dynamic_slice_in_dim(padded, start, NSEC, 0)
        site_pair = (first_op[:, None, :, None] * second_op[None, :, None, :]).reshape(SITE * SITE, SITE * SITE)
        moved = jnp.einsum('kac,kcx->kax', left_block, source.reshape(NSEC, BOND_CAP, SITE * SITE * BOND_CAP), precision=highest)
        moved = moved.reshape(NSEC, BOND_CAP, SITE * SITE, BOND_CAP)
        mixed = jnp.einsum('pq,kaqd->kapd', site_pair, moved, precision=highest)
        result = jnp.einsum('kapd,kbd->kapb', mixed, right_block, precision=highest)
        return summed + allowed.astype(summed.dtype)[:, None, None, None] * result, None

    start_sum = jnp.zeros((NSEC, BOND_CAP, SITE * SITE, BOND_CAP), jnp.float32)
    summed, unused = lax.scan(step, start_sum, (left_env, right_env, site_one, site_two, term_charge, pair_mask))
    return summed * block_mask[:, :, None, :]
```

```python
import functools

import jax
import jax.numpy as jnp
from jax import lax
from jax.experimental import pallas as pl
from jax.experimental.pallas import tpu as pltpu
from jax.sharding import PartitionSpec as P

VMEM = pl.BlockSpec(memory_space=pltpu.VMEM)
SMEM = pl.BlockSpec(memory_space=pltpu.SMEM)
LIMIT = 40 * 1024 * 1024


def split(x):
    high = x.astype(jnp.bfloat16)
    low = (x - high.astype(jnp.float32)).astype(jnp.bfloat16)
    return high, low


def local_sector(blk, first):
    odd = lax.rem(blk, 2)
    return 1 - odd if first else odd


def partner_of(z):
    return z + 1 - 2 * lax.rem(z, 2)


def apply_kernel(
    own, first, groups, rows, states, bond, site, charge_ref, allowed_ref, one_ref, two_ref, theta_ref, halo_ref, *refs
):
    if own:
        left_ref, right_ref, out_ref, source, moved, mixed = refs
    else:
        env_ref, before_ref, mine_ref, rest_ref, source, moved, mixed, total = refs
    total = out_ref if own else total
    z = lax.axis_index("mpo")
    sector = local_sector(lax.axis_index("blk"), first)
    terms = (left_ref if own else env_ref).shape[0]
    height = groups * rows
    first_term = (z if own else partner_of(z)) * terms

    for slot in range(3):
        for q in range(states):
            if slot < 2:
                block = theta_ref[slot, pl.ds(q, bond, stride=states), :]
            else:
                block = halo_ref[pl.ds(q, bond, stride=states), :]
            high, low = split(block)
            source[slot, 0:bond, q * bond : (q + 1) * bond] = high
            source[slot, bond : 2 * bond, q * bond : (q + 1) * bond] = low

    total[...] = jnp.zeros_like(total) if own else before_ref[...]

    def pair(w, carry):
        term = first_term + w

        @pl.when(allowed_ref[term, sector] != 0)
        def _():
            shifted = sector - charge_ref[term]
            slot = jnp.where((shifted >= 0) & (shifted <= 1), shifted, 2)
            if own:
                parts = []
                for r in range(groups):
                    dest = lax.rem(lax.div(z, 2) + r, groups) * 2 + lax.rem(z, 2)
                    start = pl.multiple_of(dest * rows, rows)
                    parts.append(left_ref[w, sector, pl.ds(start, rows), :])
                left = jnp.concatenate(parts, axis=0) if groups > 1 else parts[0]
                right = right_ref[w, sector]
            else:
                left = env_ref[w, 0:height, :]
                right = env_ref[w, height : height + bond, :]
            stacked = jnp.concatenate(split(left), axis=0)
            rows_in = jnp.concatenate([stacked, stacked], axis=1)
            for s in range(site):
                cut = slice(s * site * bond, (s + 1) * site * bond)
                moved[:, cut] = jnp.dot(rows_in, source[slot, :, cut], preferred_element_type=jnp.float32)
            one = [[one_ref[term, i, j] for j in range(site)] for i in range(site)]
            two = [[two_ref[term, i, j] for j in range(site)] for i in range(site)]
            step = 16
            for start in range(0, height, step):
                half = []
                for s in range(site):
                    cols = []
                    for u in range(site):
                        cut = slice((s * site + u) * bond, (s * site + u + 1) * bond)
                        cols.append(moved[start : start + step, cut] + moved[height + start : height + start + step, cut])
                    half.append([sum(two[v][u] * cols[u] for u in range(site)) for v in range(site)])
                for v in range(site):
                    for t in range(site):
                        value = sum(one[t][s] * half[s][v] for s in range(site))
                        high, low = split(value)
                        at = (t * site + v) * height + start
                        mixed[at : at + step, 0:bond] = high
                        mixed[at : at + step, bond : 2 * bond] = low
            folded = jnp.concatenate(split(right), axis=0)
            weights = jnp.concatenate([folded, folded], axis=1)
            chunk = 256
            for at in range(0, states * height, chunk):
                got = lax.dot_general(
                    mixed[at : at + chunk, :], weights, (((1,), (1,)), ((), ())), preferred_element_type=jnp.float32
                )
                total[at : at + chunk, :] += got[:, :bond] + got[:, bond:]

        return carry

    lax.fori_loop(0, terms, pair, 0)
    if not own:
        for p in range(states):
            mine_ref[p] = total[p * height : p * height + rows, :]
            for r in range(1, groups):
                at = p * height + r * rows
                rest_ref[r - 1, p] = total[at : at + rows, :]


def apply_terms(own, first, groups, rows, scalars, theta, halo, operands):
    states = 16
    bond = theta.shape[-1]
    states = theta.shape[1] // bond
    site = scalars[2].shape[-1]
    height = groups * rows
    flat = jax.ShapeDtypeStruct((states * height, bond), jnp.float32)
    scratch = [
        pltpu.VMEM((3, 2 * bond, states * bond), jnp.bfloat16),
        pltpu.VMEM((2 * height, states * bond), jnp.float32),
        pltpu.VMEM((states * height, 2 * bond), jnp.bfloat16),
    ]
    if own:
        out = flat
    else:
        out = (
            jax.ShapeDtypeStruct((states, rows, bond), jnp.float32),
            jax.ShapeDtypeStruct((groups - 1, states, rows, bond), jnp.float32),
        )
        scratch.append(pltpu.VMEM(flat.shape, jnp.float32))
    pairs = operands[0].shape[0]
    return pl.pallas_call(
        functools.partial(apply_kernel, own, first, groups, rows, states, bond, site),
        out_shape=out,
        in_specs=[SMEM] * 4 + [VMEM] * (2 + len(operands)),
        out_specs=VMEM if own else (VMEM, VMEM),
        scratch_shapes=scratch,
        compiler_params=pltpu.CompilerParams(vmem_limit_bytes=LIMIT),
        cost_estimate=pl.CostEstimate(
            flops=pairs * 8 * states * height * bond * bond, bytes_accessed=4 * 1024 * 1024, transcendentals=0
        ),
        name=("own" if own else "partner") + ("_first" if first else "_second"),
    )(*scalars, theta, halo, *operands)


def finish_kernel(rows, states, bond, dims_ref, first_ref, first_got, second_ref, second_got, out_ref):
    z = lax.axis_index("mpo")
    blk = lax.axis_index("blk")
    for first, mine, got in ((True, first_ref, first_got), (False, second_ref, second_got)):
        sector = local_sector(blk, first)
        row = lax.broadcasted_iota(jnp.int32, (rows, bond), 0) + z * rows
        col = lax.broadcasted_iota(jnp.int32, (rows, bond), 1)
        keep = ((row < dims_ref[sector, 0]) & (col < dims_ref[sector, 1])).astype(jnp.float32)
        for p in range(states):
            value = mine[p]
            for r in range(got.shape[0]):
                value = value + got[r, p]
            out_ref[sector, pl.ds(p, rows, stride=states), :] = value * keep


def body(theta, block_dims, pair_mask, term_charge, left_env, right_env, site_one, site_two):
    sectors, bond, states, _ = theta.shape
    blk, z = lax.axis_index("blk"), lax.axis_index("mpo")
    blk_count, group_count = lax.axis_size("blk"), lax.axis_size("mpo")
    terms = left_env.shape[0]
    rows = bond // group_count
    groups = group_count // 2
    scalars = (term_charge, pair_mask, site_one, site_two)
    across = partner_of(z)
    swap = [(i, i ^ 1) for i in range(group_count)]

    def packed(first):
        sector = local_sector(blk, first)
        left = lax.dynamic_index_in_dim(left_env, sector, 1, keepdims=False)
        right = lax.dynamic_index_in_dim(right_env, sector, 1, keepdims=False)
        parts = []
        for r in range(groups):
            dest = lax.rem(lax.div(z, 2) + r, groups) * 2 + lax.rem(across, 2)
            parts.append(lax.dynamic_slice_in_dim(left, dest * rows, rows, 1))
        return jnp.concatenate(parts + [right], axis=1)

    env_first = lax.ppermute(packed(True), "mpo", swap)
    env_second = lax.ppermute(packed(False), "mpo", swap)

    places = jnp.arange(bond, dtype=jnp.int32)
    left_ok = places[None, :] < block_dims[:, 0:1]
    right_ok = places[None, :] < block_dims[:, 1:2]
    keep = (left_ok[:, :, None, None] & right_ok[:, None, None, :]).astype(jnp.float32)
    masked = theta * keep
    inner = lax.dynamic_index_in_dim(masked, local_sector(blk, True), 0, keepdims=False)
    outer = lax.dynamic_index_in_dim(masked, local_sector(blk, False), 0, keepdims=False)
    pairs = blk_count // 2
    halo_first = lax.ppermute(inner, "blk", [(i, i ^ 1) for i in range(2 * pairs)])
    crossing = [(2 * i + 1, 2 * i + 2) for i in range(pairs - 1)]
    halo_second = lax.ppermute(outer, "blk", crossing + [(b, a) for a, b in crossing])

    flat = masked.reshape(sectors, bond * states, bond)
    results = []
    for first, halo, env in ((True, halo_first, env_first), (False, halo_second, env_second)):
        halo = halo.reshape(bond * states, bond)
        own = apply_terms(True, first, groups, rows, scalars, flat, halo, (left_env, right_env))
        mine, rest = apply_terms(False, first, groups, rows, scalars, flat, halo, (env, own))
        got = []
        for r in range(1, groups):
            route = [(i, ((i // 2 + r) % groups) * 2 + i % 2) for i in range(group_count)]
            got.append(lax.ppermute(rest[r - 1], "mpo", route))
        got = got[0][None] if groups == 2 else jnp.stack(got)
        results += [mine, got]

    out = pl.pallas_call(
        functools.partial(finish_kernel, rows, states, bond),
        out_shape=jax.ShapeDtypeStruct((sectors, rows * states, bond), jnp.float32),
        in_specs=[SMEM] + [VMEM] * 4,
        out_specs=VMEM,
        compiler_params=pltpu.CompilerParams(vmem_limit_bytes=LIMIT),
        name="finish",
    )(block_dims, *results)
    return out.reshape(sectors, rows, states, bond)


def solution(mesh):
    placed = (
        P("blk", None, None, None),
        P("blk", None),
        P(None, "blk"),
        P(),
        P("mpo", "blk", None, None),
        P("mpo", "blk", None, None),
        P(),
        P(),
    )
    return jax.shard_map(
        body, mesh=mesh, in_specs=placed, out_specs=P("blk", "mpo", None, None), check_vma=False
    )
```

```python
import functools

import jax
import jax.numpy as jnp
from jax import lax
from jax.experimental import pallas as pl
from jax.experimental.pallas import tpu as pltpu
from jax.sharding import PartitionSpec as P

VMEM = pl.BlockSpec(memory_space=pltpu.VMEM)
ANY = pl.BlockSpec(memory_space=pl.ANY)
LIGHT = pl.CostEstimate(flops=1, bytes_accessed=1, transcendentals=0)
PARAMS = pltpu.CompilerParams(vmem_limit_bytes=24 * 1024 * 1024)


def split(x):
    high = x.astype(jnp.bfloat16)
    low = (x - high.astype(jnp.float32)).astype(jnp.bfloat16)
    return high, low


def weighted(scales, values):
    total = scales[0] * values[0]
    for scale, value in zip(scales[1:], values[1:]):
        total = total + scale * value
    return total


def local_sector(blk, first):
    odd = lax.rem(blk, 2)
    return 1 - odd if first else odd


def partner_of(z):
    return z + 1 - 2 * lax.rem(z, 2)


def row_start(z, parity, r, groups, rows):
    dest = lax.rem(lax.div(z, 2) + r, groups) * 2 + parity
    return pl.multiple_of(dest * rows, rows)


def env_copies(first, own, groups, rows, left_ref, right_ref, env_ref, sem):
    z = lax.axis_index("mpo")
    sector = local_sector(lax.axis_index("blk"), first)
    height, bond = groups * rows, right_ref.shape[-1]
    copies = []
    for r in range(groups):
        start = row_start(z, lax.rem(z if own else partner_of(z), 2), r, groups, rows)
        source = left_ref.at[:, sector, pl.ds(start, rows), :]
        copies.append(pltpu.make_async_copy(source, env_ref.at[:, r * rows : (r + 1) * rows, :], sem.at[r]))
    source = right_ref.at[:, sector]
    copies.append(pltpu.make_async_copy(source, env_ref.at[:, height : height + bond, :], sem.at[groups]))
    return copies


def pack_kernel(first, groups, rows, left_ref, right_ref, env_ref, sem):
    copies = env_copies(first, False, groups, rows, left_ref, right_ref, env_ref, sem)
    for copy in copies:
        copy.start()
    for copy in copies:
        copy.wait()


def mask_kernel(first, states, dims_ref, theta_ref, out_ref, dims, held, sem):
    sector = local_sector(lax.axis_index("blk"), first)
    copies = [
        pltpu.make_async_copy(dims_ref, dims, sem.at[0]),
        pltpu.make_async_copy(theta_ref.at[sector], held, sem.at[1]),
    ]
    for copy in copies:
        copy.start()
    for copy in copies:
        copy.wait()
    step = 256

    def part(i, carry):
        start = pl.multiple_of(i * step, step)
        row = lax.broadcasted_iota(jnp.int32, (step, held.shape[1]), 0) + start
        col = lax.broadcasted_iota(jnp.int32, (step, held.shape[1]), 1)
        keep = (row < dims[sector, 0] * states) & (col < dims[sector, 1])
        out_ref[pl.ds(start, step), :] = jnp.where(keep, held[pl.ds(start, step), :], 0.0)
        return carry

    lax.fori_loop(0, held.shape[0] // step, part, 0)


def apply_kernel(own, first, groups, rows, bond, site, *refs):
    inputs, refs = refs[:4], refs[4:]
    if own:
        inner_ref, outer_ref, halo_ref, left_ref, right_ref, total, source, *refs = refs
        moved, mixed, charge_ref, allowed_ref, one_ref, two_ref, sem, env, env_sem, halo, halo_sem = refs
    else:
        source, env, before_ref, mine_ref, rest_ref, moved, mixed, charge_ref, allowed_ref, one_ref, two_ref, sem = refs
    scalars = (charge_ref, allowed_ref, one_ref, two_ref)
    states = site * site
    z = lax.axis_index("mpo")
    sector = local_sector(lax.axis_index("blk"), first)
    height = groups * rows
    terms = env.shape[0]
    first_term = (z if own else partner_of(z)) * terms
    block = min(rows, 16)
    joined = 16 // block

    small = [pltpu.make_async_copy(a, b, sem.at[i]) for i, (a, b) in enumerate(zip(inputs, scalars))]
    if own:
        fetch_halo = pltpu.make_async_copy(halo_ref, halo, halo_sem)
        large = env_copies(first, True, groups, rows, left_ref, right_ref, env, env_sem)
        fetch_halo.start()
    else:
        large = []
    for copy in small + large:
        copy.start()

    if own:
        total[...] = jnp.zeros_like(total)
        for slot, ref in enumerate((inner_ref, outer_ref, halo)):
            if slot == 2:
                fetch_halo.wait()

            def convert(s, carry, slot=slot, ref=ref):
                for u in range(site):
                    high, low = split(ref[pl.ds(s * site + u, bond, stride=states), :])
                    cut = pl.ds(pl.multiple_of((s * site + u) * bond, bond), bond)
                    source[slot, 0:bond, cut] = high
                    source[slot, bond : 2 * bond, cut] = low
                return carry

            lax.fori_loop(0, site, convert, 0)
    else:
        cut = mine_ref.shape[0]
        mine_ref[...] = before_ref[0:cut, :]
        rest_ref[...] = before_ref[cut:, :]
    for copy in small + large:
        copy.wait()

    def pair(w, carry):
        term = first_term + w

        @pl.when(allowed_ref[sector, term] != 0)
        def _():
            charge = charge_ref[term]
            shifted = sector - charge
            inside = (shifted >= 0) & (shifted <= 1)
            slot = jnp.where(inside, jnp.where(charge == 0, 0 if first else 1, 1 if first else 0), 2)
            stacked = jnp.concatenate(split(env[w, 0:height, :]), axis=0)
            rows_in = jnp.concatenate([stacked, stacked], axis=1)
            for s in range(site):
                cut = slice(s * site * bond, (s + 1) * site * bond)
                moved[:, cut] = jnp.dot(rows_in, source[slot, :, cut], preferred_element_type=jnp.float32)
            one = [[one_ref[i, j, term] for j in range(site)] for i in range(site)]
            two = [[two_ref[i, j, term] for j in range(site)] for i in range(site)]
            folded = jnp.concatenate(split(jnp.transpose(env[w, height : height + bond, :])), axis=1)
            weights = jnp.concatenate([folded, folded], axis=0)
            for start in range(0, height, block):
                half = []
                for s in range(site):
                    cols = []
                    for u in range(site):
                        cut = slice((s * site + u) * bond, (s * site + u + 1) * bond)
                        cols.append(moved[start : start + block, cut] + moved[height + start : height + start + block, cut])
                    half.append([weighted(two[v], cols) for v in range(site)])
                values = [weighted(one[t], [half[s][v] for s in range(site)]) for t in range(site) for v in range(site)]
                base = start * states
                for p in range(0, states, joined):
                    high, low = split(jnp.concatenate(values[p : p + joined], axis=0) if joined > 1 else values[p])
                    at = base + p * block
                    mixed[at : at + joined * block, 0:bond] = high
                    mixed[at : at + joined * block, bond : 2 * bond] = low
                got = jnp.dot(mixed[base : base + block * states, :], weights, preferred_element_type=jnp.float32)
                got = got[:, :bond] + got[:, bond:]
                if own:
                    total[base : base + block * states, :] += got
                elif start < rows:
                    mine_ref[base : base + block * states, :] += got
                else:
                    at = base - rows * states
                    rest_ref[at : at + block * states, :] += got

        return carry

    lax.fori_loop(0, terms, pair, 0)


def apply_terms(own, first, groups, rows, bond, terms, scalars, operands):
    site = scalars[2].shape[0]
    states = site * site
    height = groups * rows
    flat = jax.ShapeDtypeStruct((states * height, bond), jnp.float32)
    scratch = [
        pltpu.VMEM((2 * height, states * bond), jnp.float32),
        pltpu.VMEM((states * height, 2 * bond), jnp.bfloat16),
    ]
    scratch += [pltpu.SMEM(x.shape, x.dtype) for x in scalars]
    scratch += [pltpu.SemaphoreType.DMA((len(scalars),))]
    if own:
        out = (flat, jax.ShapeDtypeStruct((3, 2 * bond, states * bond), jnp.bfloat16))
        scratch += [pltpu.VMEM((terms, height + bond, bond), jnp.float32), pltpu.SemaphoreType.DMA((groups + 1,))]
        scratch += [pltpu.VMEM((states * bond, bond), jnp.float32), pltpu.SemaphoreType.DMA]
        places = [VMEM, VMEM, ANY, ANY, ANY]
    else:
        out = (
            jax.ShapeDtypeStruct((rows * states, bond), jnp.float32),
            jax.ShapeDtypeStruct(((groups - 1) * rows * states, bond), jnp.float32),
        )
        places = [VMEM, VMEM, VMEM]
    return pl.pallas_call(
        functools.partial(apply_kernel, own, first, groups, rows, bond, site),
        out_shape=out,
        in_specs=[ANY] * 4 + places,
        out_specs=(VMEM, VMEM),
        scratch_shapes=scratch,
        compiler_params=PARAMS,
        cost_estimate=LIGHT,
        name=("own" if own else "partner") + ("_first" if first else "_second"),
    )(*scalars, *operands)


def finish_kernel(rows, states, bond, dims_ref, *refs):
    out_ref, dims, sem = refs[-3:]
    parts = refs[:-3]
    count = len(parts) // 2
    copy = pltpu.make_async_copy(dims_ref, dims, sem)
    copy.start()
    copy.wait()
    z = lax.axis_index("mpo")
    blk = lax.axis_index("blk")
    for first, (mine, *got) in ((True, parts[:count]), (False, parts[count:])):
        sector = local_sector(blk, first)
        block = min(rows, 16)
        for start in range(0, rows, block):
            row = lax.broadcasted_iota(jnp.int32, (block, bond), 0) + (z * rows + start)
            col = lax.broadcasted_iota(jnp.int32, (block, bond), 1)
            keep = ((row < dims[sector, 0]) & (col < dims[sector, 1])).astype(jnp.float32)
            for p in range(states):
                at = (start * states) + p * block
                value = mine[at : at + block, :]
                for other in got:
                    value = value + other[at : at + block, :]
                out_ref[sector, pl.ds(start * states + p, block, stride=states), :] = value * keep


def body(theta, block_dims, pair_mask, term_charge, left_env, right_env, site_one, site_two):
    sectors, bond, states, _ = theta.shape
    blk_count, group_count = lax.axis_size("blk"), lax.axis_size("mpo")
    terms = left_env.shape[0]
    rows = bond // group_count
    groups = group_count // 2
    height = groups * rows
    scalars = (term_charge, pair_mask.T, site_one.transpose(1, 2, 0), site_two.transpose(1, 2, 0))
    swap = [(i, i ^ 1) for i in range(group_count)]

    def packed(first, left, right):
        return pl.pallas_call(
            functools.partial(pack_kernel, first, groups, rows),
            out_shape=jax.ShapeDtypeStruct((terms, height + bond, bond), jnp.float32),
            in_specs=[ANY, ANY],
            out_specs=ANY,
            scratch_shapes=[pltpu.SemaphoreType.DMA((groups + 1,))],
            compiler_params=PARAMS,
            cost_estimate=LIGHT,
            name="pack_first" if first else "pack_second",
        )(left, right)

    def masked(first, values):
        return pl.pallas_call(
            functools.partial(mask_kernel, first, states),
            out_shape=jax.ShapeDtypeStruct((bond * states, bond), jnp.float32),
            in_specs=[ANY, ANY],
            out_specs=VMEM,
            scratch_shapes=[
                pltpu.SMEM(block_dims.shape, block_dims.dtype),
                pltpu.VMEM((bond * states, bond), jnp.float32),
                pltpu.SemaphoreType.DMA((2,)),
            ],
            compiler_params=PARAMS,
            cost_estimate=LIGHT,
            name="mask_first" if first else "mask_second",
        )(block_dims, values)

    flat = pltpu.with_memory_space_constraint(theta.reshape(sectors, bond * states, bond), pltpu.HBM)
    left_env = pltpu.with_memory_space_constraint(left_env, pltpu.HBM)
    right_env = pltpu.with_memory_space_constraint(right_env, pltpu.HBM)
    pairs = blk_count // 2
    crossing = [(2 * i + 1, 2 * i + 2) for i in range(pairs - 1)]
    first_packed = packed(True, left_env, right_env)
    first_packed, flat = lax.optimization_barrier((first_packed, flat))
    env_first = lax.ppermute(first_packed, "mpo", swap)
    outer = masked(False, flat)
    outer, flat = lax.optimization_barrier((outer, flat))
    halo_second = lax.ppermute(outer, "blk", crossing + [(b, a) for a, b in crossing])
    inner = masked(True, flat)
    inner, left_tied, right_tied = lax.optimization_barrier((inner, left_env, right_env))
    halo_first = lax.ppermute(inner, "blk", [(i, i ^ 1) for i in range(2 * pairs)])
    second_packed = packed(False, left_tied, right_tied)
    env_second = lax.ppermute(second_packed, "mpo", swap)

    results = []
    for first, halo, env in ((True, halo_first, env_first), (False, halo_second, env_second)):
        if not first:
            results[0], halo = lax.optimization_barrier((results[0], halo))
        before, source = apply_terms(
            True, first, groups, rows, bond, terms, scalars, (inner, outer, halo, left_env, right_env)
        )
        mine, rest = apply_terms(False, first, groups, rows, bond, terms, scalars, (source, env, before))
        results.append(mine)
        for r in range(1, groups):
            route = [(i, ((i // 2 + r) % groups) * 2 + i % 2) for i in range(group_count)]
            cut = rows * states
            part = rest[(r - 1) * cut : r * cut]
            if not first:
                results[r], part = lax.optimization_barrier((results[r], part))
            results.append(lax.ppermute(part, "mpo", route))

    out = pl.pallas_call(
        functools.partial(finish_kernel, rows, states, bond),
        out_shape=jax.ShapeDtypeStruct((sectors, rows * states, bond), jnp.float32),
        in_specs=[ANY] + [VMEM] * len(results),
        out_specs=VMEM,
        scratch_shapes=[pltpu.SMEM(block_dims.shape, block_dims.dtype), pltpu.SemaphoreType.DMA],
        compiler_params=PARAMS,
        name="finish",
    )(block_dims, *results)
    return out.reshape(sectors, rows, states, bond)


def solution(mesh):
    placed = (
        P("blk", None, None, None),
        P("blk", None),
        P(None, "blk"),
        P(),
        P("mpo", "blk", None, None),
        P("mpo", "blk", None, None),
        P(),
        P(),
    )
    return jax.shard_map(
        body, mesh=mesh, in_specs=placed, out_specs=P("blk", "mpo", None, None), check_vma=False
    )
```

```python
import functools

import jax
import jax.numpy as jnp
from jax import lax
from jax.experimental import pallas as pl
from jax.experimental.pallas import tpu as pltpu
from jax.sharding import PartitionSpec as P

VMEM = pl.BlockSpec(memory_space=pltpu.VMEM)
ANY = pl.BlockSpec(memory_space=pl.ANY)
PARAMS = pltpu.CompilerParams(vmem_limit_bytes=24 * 1024 * 1024)
LIGHT = pl.CostEstimate(flops=1, bytes_accessed=1, transcendentals=0)
HEAVY = pl.CostEstimate(flops=10**10, bytes_accessed=1, transcendentals=0)


def split(x):
    high = x.astype(jnp.bfloat16)
    low = (x - high.astype(jnp.float32)).astype(jnp.bfloat16)
    return high, low


def weighted(scales, values):
    total = scales[0] * values[0]
    for scale, value in zip(scales[1:], values[1:]):
        total = total + scale * value
    return total


def local_sector(blk, first):
    odd = lax.rem(blk, 2)
    return 1 - odd if first else odd


def partner_of(z):
    return z + 1 - 2 * lax.rem(z, 2)


def row_start(z, parity, r, groups, rows):
    dest = lax.rem(lax.div(z, 2) + r, groups) * 2 + parity
    return pl.multiple_of(dest * rows, rows)


def env_copies(first, own, groups, rows, left_ref, right_ref, env_ref, sem):
    z = lax.axis_index("mpo")
    sector = local_sector(lax.axis_index("blk"), first)
    height, bond = groups * rows, right_ref.shape[-1]
    copies = []
    for r in range(groups):
        start = row_start(z, lax.rem(z if own else partner_of(z), 2), r, groups, rows)
        source = left_ref.at[:, sector, pl.ds(start, rows), :]
        copies.append(pltpu.make_async_copy(source, env_ref.at[:, r * rows : (r + 1) * rows, :], sem.at[r]))
    source = right_ref.at[:, sector]
    copies.append(pltpu.make_async_copy(source, env_ref.at[:, height : height + bond, :], sem.at[groups]))
    return copies


def front_kernel(leading, groups, rows, states, dims_ref, theta_ref, left_ref, right_ref, env_ref, out_ref, *scratch):
    dims, held, sem, env_sem = scratch
    sector = local_sector(lax.axis_index("blk"), leading)
    fetches = [
        pltpu.make_async_copy(dims_ref, dims, sem.at[0]),
        pltpu.make_async_copy(theta_ref.at[sector], held, sem.at[1]),
    ]
    copies = env_copies(leading, False, groups, rows, left_ref, right_ref, env_ref, env_sem)
    for copy in fetches + copies:
        copy.start()
    for copy in fetches:
        copy.wait()
    step = 256

    def part(j, carry):
        start = pl.multiple_of(j * step, step)
        row = lax.broadcasted_iota(jnp.int32, (step, held.shape[1]), 0) + start
        col = lax.broadcasted_iota(jnp.int32, (step, held.shape[1]), 1)
        keep = (row < dims[sector, 0] * states) & (col < dims[sector, 1])
        out_ref[pl.ds(start, step), :] = jnp.where(keep, held[pl.ds(start, step), :], 0.0)
        return carry

    lax.fori_loop(0, held.shape[0] // step, part, 0)
    for copy in copies:
        copy.wait()


def apply_kernel(own, first, span, groups, rows, bond, site, *refs):
    inputs, refs = refs[:4], list(refs[4:])
    take = lambda count: [refs.pop(0) for _ in range(count)]
    late = not own and not first
    if own:
        blocks = take(3 if first else 2)
        left_ref, right_ref, total, source = take(4)
    else:
        source, env, before_ref = take(3)
        if late:
            blocks = take(1)
            left_ref, right_ref = take(2)
        outs = take(2 if first else 1)
    moved, mixed, charge_ref, allowed_ref, one_ref, two_ref, sem = take(7)
    if own or late:
        own_env, env_sem = take(2)
    if late:
        kept, source, kept_sem = source, *take(2)
    states = site * site
    z = lax.axis_index("mpo")
    sector = local_sector(lax.axis_index("blk"), first)
    height = groups * rows
    low, high = span
    block = min(rows, 16)
    joined = 16 // block

    copies = [
        pltpu.make_async_copy(a, b, sem.at[i]) for i, (a, b) in enumerate(zip(inputs, (charge_ref, allowed_ref, one_ref, two_ref)))
    ]
    envs = env_copies(first, True, groups, rows, left_ref, right_ref, own_env, env_sem) if own or late else []
    if late:
        copies.append(pltpu.make_async_copy(kept.at[0:2], source.at[0:2], kept_sem))
    for copy in copies + envs:
        copy.start()

    def convert(slot, ref):
        def part(s, carry):
            for u in range(site):
                high, low = split(ref[pl.ds(s * site + u, bond, stride=states), :])
                cut = pl.ds(pl.multiple_of((s * site + u) * bond, bond), bond)
                source[slot, 0:bond, cut] = high
                source[slot, bond : 2 * bond, cut] = low
            return carry

        lax.fori_loop(0, site, part, 0)

    if own:
        total[...] = jnp.zeros_like(total)
        for slot, ref in enumerate(blocks):
            convert(slot, ref)
    else:
        at = low * states
        for out in outs:
            out[...] = before_ref[at : at + out.shape[0], :]
            at += out.shape[0]
    if late:
        convert(2, blocks[0])
    for copy in copies:
        copy.wait()

    def add_term(env, w, term, slot):
        left = env[w, low:high, :]
        left_rest = left - left.astype(jnp.bfloat16).astype(jnp.float32)
        stacked = jnp.concatenate([left, left_rest], axis=0).astype(jnp.bfloat16)
        rows_in = jnp.concatenate([stacked, stacked], axis=1)
        for s in range(site):
            cut = slice(s * site * bond, (s + 1) * site * bond)
            moved[:, cut] = jnp.dot(rows_in, source[slot, :, cut], preferred_element_type=jnp.float32)
        one = [[one_ref[i, j, term] for j in range(site)] for i in range(site)]
        two = [[two_ref[i, j, term] for j in range(site)] for i in range(site)]
        folded = jnp.concatenate(split(jnp.transpose(env[w, height : height + bond, :])), axis=1)
        weights = jnp.concatenate([folded, folded], axis=0)
        tall = high - low
        for start in range(0, tall, block):
            half = []
            for s in range(site):
                cols = []
                for u in range(site):
                    cut = slice((s * site + u) * bond, (s * site + u + 1) * bond)
                    cols.append(moved[start : start + block, cut] + moved[tall + start : tall + start + block, cut])
                half.append([weighted(two[v], cols) for v in range(site)])
            values = [weighted(one[t], [half[s][v] for s in range(site)]) for t in range(site) for v in range(site)]
            base = start * states
            for p in range(0, states, joined):
                upper, lower = split(jnp.concatenate(values[p : p + joined], axis=0) if joined > 1 else values[p])
                at = base + p * block
                mixed[at : at + joined * block, 0:bond] = upper
                mixed[at : at + joined * block, bond : 2 * bond] = lower
            got = jnp.dot(mixed[base : base + block * states, :], weights, preferred_element_type=jnp.float32)
            got = got[:, :bond] + got[:, bond:]
            if own:
                total[base : base + block * states, :] += got
            elif base < outs[0].shape[0]:
                outs[0][base : base + block * states, :] += got
            else:
                at = base - outs[0].shape[0]
                outs[1][at : at + block * states, :] += got

    def add_terms(env, owner, wanted):
        first_term = owner * env.shape[0]

        def one_term(w, carry):
            term = first_term + w
            charge = charge_ref[term]
            shifted = sector - charge
            inside = (shifted >= 0) & (shifted <= 1)
            slot = jnp.where(inside, jnp.where(charge == 0, 0 if first else 1, 1 if first else 0), 2)

            @pl.when((allowed_ref[sector, term] != 0) & wanted(slot))
            def _():
                add_term(env, w, term, slot)

            return carry

        lax.fori_loop(0, env.shape[0], one_term, 0)

    if not own:
        add_terms(env, partner_of(z), lambda slot: slot >= 0)
    for copy in envs:
        copy.wait()
    if own or late:
        add_terms(own_env, z, lambda slot: slot == 2 if late else slot <= (2 if first else 1))


def apply_terms(own, first, span, groups, rows, bond, terms, scalars, operands):
    site = scalars[2].shape[0]
    states = site * site
    height = groups * rows
    late = not own and not first
    held = jax.ShapeDtypeStruct((3, 2 * bond, states * bond), jnp.bfloat16)
    scratch = [
        pltpu.VMEM((2 * (span[1] - span[0]), states * bond), jnp.float32),
        pltpu.VMEM((states * (span[1] - span[0]), 2 * bond), jnp.bfloat16),
    ]
    scratch += [pltpu.SMEM(x.shape, x.dtype) for x in scalars]
    scratch += [pltpu.SemaphoreType.DMA((len(scalars),))]
    if own or late:
        scratch += [pltpu.VMEM((terms, height + bond, bond), jnp.float32), pltpu.SemaphoreType.DMA((groups + 1,))]
    if late:
        scratch += [pltpu.VMEM(held.shape, held.dtype), pltpu.SemaphoreType.DMA]
    if own:
        out = (jax.ShapeDtypeStruct((states * height, bond), jnp.float32), held)
        places = [VMEM] * (len(operands) - 2) + [ANY, ANY]
    else:
        cuts = [(0, rows), (rows, height)] if first else [span]
        out = tuple(jax.ShapeDtypeStruct(((b - a) * states, bond), jnp.float32) for a, b in cuts)
        places = [ANY, VMEM, VMEM, VMEM, ANY, ANY] if late else [VMEM] * 3
    return pl.pallas_call(
        functools.partial(apply_kernel, own, first, span, groups, rows, bond, site),
        out_shape=out,
        in_specs=[ANY] * 4 + places,
        out_specs=(VMEM,) * len(out),
        scratch_shapes=scratch,
        compiler_params=PARAMS,
        cost_estimate=HEAVY if own and first else LIGHT,
        name=("own" if own else "partner") + ("_first" if first else "_second" if own else f"_second_{span[0]}"),
    )(*scalars, *operands)


def finish_kernel(first, rows, states, bond, *refs):
    if first:
        dims_ref, *parts, out_ref, keep_ref, held, sem, dims = refs
        copy = pltpu.make_async_copy(dims_ref, dims, sem.at[1])
        copy.start()
        copy.wait()
    else:
        _, keep_ref, *parts, out_ref, held, sem = refs
    blk = lax.axis_index("blk")
    sector = local_sector(blk, first)
    block = min(rows, 16)

    def mask(sector, start):
        row = lax.broadcasted_iota(jnp.int32, (block, bond), 0) + (lax.axis_index("mpo") * rows + start)
        col = lax.broadcasted_iota(jnp.int32, (block, bond), 1)
        return ((row < dims[sector, 0]) & (col < dims[sector, 1])).astype(jnp.float32)

    for start in range(0, rows, block):
        if first:
            keep = mask(sector, start)
            keep_ref[start : start + block, :] = mask(local_sector(blk, False), start)
        else:
            keep = keep_ref[start : start + block, :]
        for p in range(states):
            at = start * states + p * block
            value = parts[0][at : at + block, :]
            for other in parts[1:]:
                value = value + other[at : at + block, :]
            held[pl.ds(start * states + p, block, stride=states), :] = value * keep
    copy = pltpu.make_async_copy(held, out_ref.at[sector], sem.at[0])
    copy.start()
    copy.wait()


def body(theta, block_dims, pair_mask, term_charge, left_env, right_env, site_one, site_two):
    sectors, bond, states, _ = theta.shape
    blk_count, group_count = lax.axis_size("blk"), lax.axis_size("mpo")
    terms = left_env.shape[0]
    rows = bond // group_count
    groups = group_count // 2
    height = groups * rows
    scalars = (term_charge, pair_mask.T, site_one.transpose(1, 2, 0), site_two.transpose(1, 2, 0))
    swap = [(i, i ^ 1) for i in range(group_count)]
    flat = pltpu.with_memory_space_constraint(theta.reshape(sectors, bond * states, bond), pltpu.HBM)
    left_env = pltpu.with_memory_space_constraint(left_env, pltpu.HBM)
    right_env = pltpu.with_memory_space_constraint(right_env, pltpu.HBM)
    dims = pltpu.with_memory_space_constraint(block_dims, pltpu.HBM)

    packet = jax.ShapeDtypeStruct((terms, height + bond, bond), jnp.float32)
    sector_block = jax.ShapeDtypeStruct((bond * states, bond), jnp.float32)
    def stage(leading, *args):
        return pl.pallas_call(
            functools.partial(front_kernel, leading, groups, rows, states),
            out_shape=(packet, sector_block),
            in_specs=[ANY] * 4,
            out_specs=(VMEM, VMEM),
            scratch_shapes=[
                pltpu.SMEM(block_dims.shape, block_dims.dtype),
                pltpu.VMEM((bond * states, bond), jnp.float32),
                pltpu.SemaphoreType.DMA((2,)),
                pltpu.SemaphoreType.DMA((groups + 1,)),
            ],
            compiler_params=PARAMS,
            cost_estimate=LIGHT,
            name="front_first" if leading else "front_second",
        )(*args)

    first_packed, inner = stage(True, dims, flat, left_env, right_env)
    first_packed, inner, dims, flat, left_env, right_env = lax.optimization_barrier((first_packed, inner, dims, flat, left_env, right_env))
    second_packed, outer = stage(False, dims, flat, left_env, right_env)
    pairs = blk_count // 2
    crossing = [(2 * i + 1, 2 * i + 2) for i in range(pairs - 1)]
    env_first = lax.ppermute(first_packed, "mpo", swap)
    halo_second = lax.ppermute(outer, "blk", crossing + [(b, a) for a, b in crossing])
    halo_first = lax.ppermute(inner, "blk", [(i, i ^ 1) for i in range(2 * pairs)])
    env_second = lax.ppermute(second_packed, "mpo", swap)

    shared = (groups, rows, bond, terms, scalars)
    whole, mine, rest = (0, height), (0, rows), (rows, height)
    before, source = apply_terms(True, True, whole, *shared, (inner, outer, halo_first, left_env, right_env))
    first_mine, first_rest = apply_terms(False, True, whole, *shared, (source, env_first, before))
    first_mine, outer = lax.optimization_barrier((first_mine, outer))
    before, source = apply_terms(True, False, whole, *shared, (inner, outer, left_env, right_env))
    late = (source, env_second, before, halo_second, left_env, right_env)
    (second_rest,) = apply_terms(False, False, rest, *shared, late)

    first_parts, second_parts = [], []
    cut = rows * states
    for r in range(1, groups):
        route = [(i, ((i // 2 + r) % groups) * 2 + i % 2) for i in range(group_count)]
        arrived = lax.ppermute(first_rest[(r - 1) * cut : r * cut], "mpo", route)
        arrived, leaving = lax.optimization_barrier((arrived, second_rest[(r - 1) * cut : r * cut]))
        first_parts.append(arrived)
        second_parts.append(lax.ppermute(leaving, "mpo", route))
    late = lax.optimization_barrier((*late, second_rest))[:-1]
    (second_mine,) = apply_terms(False, False, mine, *shared, late)

    def finish(first, *operands):
        out = jax.ShapeDtypeStruct((sectors, rows * states, bond), jnp.float32)
        keep = jax.ShapeDtypeStruct((rows, bond), jnp.float32)
        scratch = [pltpu.VMEM((rows * states, bond), jnp.float32), pltpu.SemaphoreType.DMA((2,))]
        if first:
            scratch.append(pltpu.SMEM(block_dims.shape, block_dims.dtype))
        return pl.pallas_call(
            functools.partial(finish_kernel, first, rows, states, bond),
            out_shape=(out, keep) if first else out,
            in_specs=[ANY] + [VMEM] * (len(operands) - 1),
            out_specs=(ANY, VMEM) if first else ANY,
            scratch_shapes=scratch,
            input_output_aliases={} if first else {0: 0},
            compiler_params=PARAMS,
            cost_estimate=LIGHT,
            name="finish_first" if first else "finish_second",
        )(*operands)

    out, keep = finish(True, dims, first_mine, *first_parts)
    out = finish(False, out, keep, second_mine, *second_parts)
    return out.reshape(sectors, rows, states, bond)


def solution(mesh):
    placed = (
        P("blk", None, None, None),
        P("blk", None),
        P(None, "blk"),
        P(),
        P("mpo", "blk", None, None),
        P("mpo", "blk", None, None),
        P(),
        P(),
    )
    return jax.shard_map(
        body, mesh=mesh, in_specs=placed, out_specs=P("blk", "mpo", None, None), check_vma=False
    )
```

```python
import functools

import jax
import jax.numpy as jnp
from jax import lax
from jax.experimental import pallas as pl
from jax.experimental.pallas import tpu as pltpu
from jax.sharding import PartitionSpec as P

VMEM = pl.BlockSpec(memory_space=pltpu.VMEM)
ANY = pl.BlockSpec(memory_space=pl.ANY)
PARAMS = pltpu.CompilerParams(vmem_limit_bytes=24 * 1024 * 1024)
LIGHT = pl.CostEstimate(flops=1, bytes_accessed=1, transcendentals=0)


def split(x):
    high = x.astype(jnp.bfloat16)
    low = (x - high.astype(jnp.float32)).astype(jnp.bfloat16)
    return high, low


def weighted(scales, values):
    total = scales[0] * values[0]
    for scale, value in zip(scales[1:], values[1:]):
        total = total + scale * value
    return total


def local_sector(blk, first):
    odd = lax.rem(blk, 2)
    return 1 - odd if first else odd


def partner_of(z):
    return z + 1 - 2 * lax.rem(z, 2)


def row_start(z, parity, r, groups, rows):
    dest = lax.rem(lax.div(z, 2) + r, groups) * 2 + parity
    return pl.multiple_of(dest * rows, rows)


def env_copies(first, sides, groups, rows, left_ref, right_ref, env_ref, sem, skip=0):
    z = lax.axis_index("mpo")
    some = slice(skip, skip + env_ref.shape[0])
    sector = local_sector(lax.axis_index("blk"), first)
    bond = right_ref.shape[-1]
    copies, at = [], 0
    for own in sides:
        for r in range(groups):
            start = row_start(z, lax.rem(z if own else partner_of(z), 2), r, groups, rows)
            source = left_ref.at[some, sector, pl.ds(start, rows), :]
            copies.append(pltpu.make_async_copy(source, env_ref.at[:, at : at + rows, :], sem.at[len(copies)]))
            at += rows
    source = right_ref.at[some, sector]
    copies.append(pltpu.make_async_copy(source, env_ref.at[:, at : at + bond, :], sem.at[len(copies)]))
    return copies


def front_kernel(groups, rows, states, dims_ref, theta_ref, left_ref, right_ref, *refs):
    outer_ref, inner_ref, early_ref, last_ref, dims, held, sem, early_sem, last_sem = refs
    blk = lax.axis_index("blk")
    fetches = [pltpu.make_async_copy(dims_ref, dims, sem.at[2])]
    for i, first in enumerate((False, True)):
        fetches.append(pltpu.make_async_copy(theta_ref.at[local_sector(blk, first)], held.at[i], sem.at[i]))
    copies = env_copies(False, (False,), groups, rows, left_ref, right_ref, early_ref, early_sem)
    copies += env_copies(False, (False,), groups, rows, left_ref, right_ref, last_ref, last_sem, early_ref.shape[0])
    for copy in fetches + copies:
        copy.start()
    step = 256
    fetches[0].wait()
    for i, (first, out_ref) in enumerate(((False, outer_ref), (True, inner_ref))):
        sector = local_sector(blk, first)
        fetches[i + 1].wait()

        def part(j, carry, i=i, out_ref=out_ref, sector=sector):
            start = pl.multiple_of(j * step, step)
            row = lax.broadcasted_iota(jnp.int32, (step, held.shape[2]), 0) + start
            col = lax.broadcasted_iota(jnp.int32, (step, held.shape[2]), 1)
            keep = (row < dims[sector, 0] * states) & (col < dims[sector, 1])
            out_ref[pl.ds(start, step), :] = jnp.where(keep, held[i, pl.ds(start, step), :], 0.0)
            return carry

        lax.fori_loop(0, held.shape[1] // step, part, 0)
    for copy in copies:
        copy.wait()


class Call:
    def __init__(self, name, first, cuts, slots=(), own=(), packets=(), added=False, near=None):
        self.name, self.first, self.cuts, self.slots = name, first, cuts, slots
        self.own, self.packets, self.added, self.near = own, packets, added, near
        self.leads = 0 in slots
        self.far = slots == (2,)
        self.kept = not slots


def apply_kernel(call, groups, rows, bond, site, terms, *refs):
    refs = list(refs)
    take = lambda count: [refs.pop(0) for _ in range(count)]
    table_refs = take(4)
    blocks = take(len(call.slots))
    source = take(1)[0] if call.kept else None
    left_ref, right_ref = take(2) if call.own else (None, None)
    packets = take(len(call.packets))
    before_ref = take(1)[0] if call.added else None
    outs = take(len(call.cuts))
    if call.slots:
        source = take(1)[0]
    moved, mixed, charge_ref, allowed_ref, one_ref, two_ref, sem = take(7)
    states = site * site
    z = lax.axis_index("mpo")
    sector = local_sector(lax.axis_index("blk"), call.first)
    low, high = call.cuts[0][0], call.cuts[-1][1]
    tall = high - low
    block = min(rows, 16)
    joined = 16 // block

    tables = (charge_ref, allowed_ref, one_ref, two_ref)
    copies = [pltpu.make_async_copy(a, b, sem.at[i]) for i, (a, b) in enumerate(zip(table_refs, tables))]
    sides = [(packet, partner_of(z) * terms + skip) for packet, skip in zip(packets, call.packets)]
    if call.own:
        env, env_sem = take(2)
        copies += env_copies(call.first, call.own, groups, rows, left_ref, right_ref, env, env_sem)
        sides.append((env, z * terms))
    for copy in copies:
        copy.start()

    for i, ref in enumerate(blocks):

        def part(s, carry, i=i, ref=ref):
            for u in range(site):
                upper, lower = split(ref[pl.ds(s * site + u, bond, stride=states), :])
                cut = pl.ds(pl.multiple_of((s * site + u) * bond, bond), bond)
                source[i, 0:bond, cut] = upper
                source[i, bond : 2 * bond, cut] = lower
            return carry

        lax.fori_loop(0, site, part, 0)

    at = low * states
    for out in outs:
        out[...] = before_ref[at : at + out.shape[0], :] if call.added else jnp.zeros_like(out)
        at += out.shape[0]
    for copy in copies:
        copy.wait()

    def add_term(env, w, term, slot):
        left = env[w, low:high, :]
        left_rest = left - left.astype(jnp.bfloat16).astype(jnp.float32)
        stacked = jnp.concatenate([left, left_rest], axis=0).astype(jnp.bfloat16)
        rows_in = jnp.concatenate([stacked, stacked], axis=1)
        for s in range(site):
            cut = slice(s * site * bond, (s + 1) * site * bond)
            moved[:, cut] = jnp.dot(rows_in, source[slot, :, cut], preferred_element_type=jnp.float32)
        one = [[one_ref[i, j, term] for j in range(site)] for i in range(site)]
        two = [[two_ref[i, j, term] for j in range(site)] for i in range(site)]
        right = env[w, env.shape[1] - bond :, :]
        folded = jnp.concatenate(split(jnp.transpose(right)), axis=1)
        weights = jnp.concatenate([folded, folded], axis=0)
        for start in range(0, tall, block):
            half = []
            for s in range(site):
                cols = []
                for u in range(site):
                    cut = slice((s * site + u) * bond, (s * site + u + 1) * bond)
                    cols.append(moved[start : start + block, cut] + moved[tall + start : tall + start + block, cut])
                half.append([weighted(two[v], cols) for v in range(site)])
            values = [weighted(one[t], [half[s][v] for s in range(site)]) for t in range(site) for v in range(site)]
            base, size = start * states, block * states
            for p in range(0, states, joined):
                upper, lower = split(jnp.concatenate(values[p : p + joined], axis=0) if joined > 1 else values[p])
                here = base + p * block
                mixed[here : here + joined * block, 0:bond] = upper
                mixed[here : here + joined * block, bond : 2 * bond] = lower
            got = jnp.dot(mixed[base : base + size, :], weights, preferred_element_type=jnp.float32)
            got = got[:, :bond] + got[:, bond:]
            for (first_row, last_row), out in zip(call.cuts, outs):
                if first_row <= low + start < last_row:
                    at = (low + start - first_row) * states
                    out[at : at + size, :] += got

    for env, first_term in sides:

        def one_term(w, carry, env=env, first_term=first_term):
            term = first_term + w
            charge = charge_ref[term]
            shifted = sector - charge
            inside = (shifted >= 0) & (shifted <= 1)
            wanted = allowed_ref[sector, term] != 0
            if call.near is not None:
                wanted = wanted & (inside if call.near else jnp.logical_not(inside))
            if call.far:
                slot = 0
            else:
                slot = jnp.where(inside, jnp.where(charge == 0, 0 if call.first else 1, 1 if call.first else 0), 2)

            @pl.when(wanted)
            def _():
                add_term(env, w, term, slot)

            return carry

        lax.fori_loop(0, env.shape[0], one_term, 0)


def apply_terms(call, sizes, tables, operands):
    groups, rows, bond, site, terms = sizes
    states = site * site
    height = groups * rows
    tall = call.cuts[-1][1] - call.cuts[0][0]
    scratch = [
        pltpu.VMEM((2 * tall, states * bond), jnp.float32),
        pltpu.VMEM((states * tall, 2 * bond), jnp.bfloat16),
    ]
    scratch += [pltpu.SMEM(x.shape, x.dtype) for x in tables]
    scratch.append(pltpu.SemaphoreType.DMA((len(tables),)))
    places = [ANY] * 4 + [VMEM] * (len(call.slots) + call.kept)
    if call.own:
        places += [ANY, ANY]
        count = len(call.own)
        scratch.append(pltpu.VMEM((terms, count * height + bond, bond), jnp.float32))
        scratch.append(pltpu.SemaphoreType.DMA((count * groups + 1,)))
    places += [VMEM] * (len(call.packets) + call.added)
    out = [jax.ShapeDtypeStruct(((b - a) * states, bond), jnp.float32) for a, b in call.cuts]
    shape = (len(call.slots), 2 * bond, states * bond)
    if call.leads:
        out.append(jax.ShapeDtypeStruct(shape, jnp.bfloat16))
    elif call.slots:
        scratch.insert(0, pltpu.VMEM(shape, jnp.bfloat16))
    return pl.pallas_call(
        functools.partial(apply_kernel, call, *sizes),
        out_shape=tuple(out),
        in_specs=places,
        out_specs=(VMEM,) * len(out),
        scratch_shapes=scratch,
        compiler_params=PARAMS,
        cost_estimate=LIGHT,
        name=call.name,
    )(*tables, *operands)


def join_kernel(mine_ref, got_ref, out_ref):
    out_ref[...] = mine_ref[...] + got_ref[...]


def finish_kernel(first, rows, states, bond, *refs):
    if first:
        dims_ref, *parts, out_ref, keep_ref, held, sem, dims = refs
        copy = pltpu.make_async_copy(dims_ref, dims, sem.at[1])
        copy.start()
        copy.wait()
    else:
        _, keep_ref, *parts, out_ref, held, sem = refs
    blk = lax.axis_index("blk")
    sector = local_sector(blk, first)
    block = min(rows, 16)

    def mask(sector, start):
        row = lax.broadcasted_iota(jnp.int32, (block, bond), 0) + (lax.axis_index("mpo") * rows + start)
        col = lax.broadcasted_iota(jnp.int32, (block, bond), 1)
        return ((row < dims[sector, 0]) & (col < dims[sector, 1])).astype(jnp.float32)

    for start in range(0, rows, block):
        if first:
            keep = mask(sector, start)
            keep_ref[start : start + block, :] = mask(local_sector(blk, False), start)
        else:
            keep = keep_ref[start : start + block, :]
        for p in range(states):
            at = start * states + p * block
            value = parts[0][at : at + block, :]
            for other in parts[1:]:
                value = value + other[at : at + block, :]
            held[pl.ds(start * states + p, block, stride=states), :] = value * keep
    copy = pltpu.make_async_copy(held, out_ref.at[sector], sem.at[0])
    copy.start()
    copy.wait()


def body(theta, block_dims, pair_mask, term_charge, left_env, right_env, site_one, site_two):
    sectors, bond, states, _ = theta.shape
    blk_count, group_count = lax.axis_size("blk"), lax.axis_size("mpo")
    terms = left_env.shape[0]
    rows = bond // group_count
    groups = group_count // 2
    height = groups * rows
    swap = [(i, i ^ 1) for i in range(group_count)]
    flat = pltpu.with_memory_space_constraint(theta.reshape(sectors, bond * states, bond), pltpu.HBM)
    left_env = pltpu.with_memory_space_constraint(left_env, pltpu.HBM)
    right_env = pltpu.with_memory_space_constraint(right_env, pltpu.HBM)
    dims = pltpu.with_memory_space_constraint(block_dims, pltpu.HBM)

    sector_block = jax.ShapeDtypeStruct((bond * states, bond), jnp.float32)
    last = max(terms // 3, 1)
    early = terms - last
    packets = [jax.ShapeDtypeStruct((count, height + bond, bond), jnp.float32) for count in (early, last)]

    outer, inner, early_packed, last_packed = pl.pallas_call(
        functools.partial(front_kernel, groups, rows, states),
        out_shape=(sector_block, sector_block, *packets),
        in_specs=[ANY] * 4,
        out_specs=(VMEM,) * 4,
        scratch_shapes=[
            pltpu.SMEM(block_dims.shape, block_dims.dtype),
            pltpu.VMEM((2, bond * states, bond), jnp.float32),
            pltpu.SemaphoreType.DMA((3,)),
            pltpu.SemaphoreType.DMA((groups + 1,)),
            pltpu.SemaphoreType.DMA((groups + 1,)),
        ],
        compiler_params=PARAMS,
        cost_estimate=LIGHT,
        name="front",
    )(dims, flat, left_env, right_env)
    tables = (term_charge, pair_mask.T, site_one.transpose(1, 2, 0), site_two.transpose(1, 2, 0))
    pairs = blk_count // 2
    crossing = [(2 * i + 1, 2 * i + 2) for i in range(pairs - 1)]
    halo_second = lax.ppermute(outer, "blk", crossing + [(b, a) for a, b in crossing])
    halo_first = lax.ppermute(inner, "blk", [(i, i ^ 1) for i in range(2 * pairs)])
    early_env = lax.ppermute(early_packed, "mpo", swap)

    sizes = (groups, rows, bond, site_one.shape[-1], terms)
    every, mine, rest = [(0, height)], [(0, rows)], [(rows, height)]
    theirs = [(height, height + rows), (height + rows, 2 * height)]
    envs = (left_env, right_env)

    call = Call("first_own", True, mine + rest + theirs, slots=(0, 1, 2), own=(True, False))
    operands = (inner, outer, halo_first, *envs)
    first_mine, first_rest, mine_away, rest_away, source = apply_terms(call, sizes, tables, operands)
    rest_away, last_packed = lax.optimization_barrier((rest_away, last_packed))
    rest_got = lax.ppermute(rest_away, "mpo", swap)
    last_env = lax.ppermute(last_packed, "mpo", swap)
    call = Call("second_near", False, every, own=(True,), packets=(0,), near=True)
    (before,) = apply_terms(call, sizes, tables, (source, *envs, early_env))
    rest_got, before = lax.optimization_barrier((rest_got, before))
    first_rest = pl.pallas_call(
        join_kernel,
        out_shape=jax.ShapeDtypeStruct(first_rest.shape, first_rest.dtype),
        in_specs=[VMEM] * 2,
        out_specs=VMEM,
        compiler_params=PARAMS,
        cost_estimate=LIGHT,
        name="join",
    )(first_rest, rest_got)
    first_rest, before = lax.optimization_barrier((first_rest, before))
    call = Call("second_last", False, every, packets=(early,), added=True, near=True)
    (before,) = apply_terms(call, sizes, tables, (source, last_env, before))
    before, mine_away = lax.optimization_barrier((before, mine_away))
    mine_got = lax.ppermute(mine_away, "mpo", swap)
    operands = (halo_second, *envs, early_env, last_env, before)
    far = dict(slots=(2,), own=(True,), packets=(0, early), added=True, near=False)
    call = Call("second_rest", False, rest, **far)
    (second_rest,) = apply_terms(call, sizes, tables, operands)

    first_parts, second_parts = [mine_got], []
    cut = rows * states
    for r in range(1, groups):
        route = [(i, ((i // 2 + r) % groups) * 2 + i % 2) for i in range(group_count)]
        first_parts.append(lax.ppermute(first_rest[(r - 1) * cut : r * cut], "mpo", route))
        second_parts.append(lax.ppermute(second_rest[(r - 1) * cut : r * cut], "mpo", route))

    def finish(first, *operands):
        out = jax.ShapeDtypeStruct((sectors, rows * states, bond), jnp.float32)
        keep = jax.ShapeDtypeStruct((rows, bond), jnp.float32)
        scratch = [pltpu.VMEM((rows * states, bond), jnp.float32), pltpu.SemaphoreType.DMA((2,))]
        if first:
            scratch.append(pltpu.SMEM(block_dims.shape, block_dims.dtype))
        return pl.pallas_call(
            functools.partial(finish_kernel, first, rows, states, bond),
            out_shape=(out, keep) if first else out,
            in_specs=[ANY] + [VMEM] * (len(operands) - 1),
            out_specs=(ANY, VMEM) if first else ANY,
            scratch_shapes=scratch,
            input_output_aliases={} if first else {0: 0},
            compiler_params=PARAMS,
            cost_estimate=LIGHT,
            name="finish_first" if first else "finish_second",
        )(*operands)

    first_parts[1], *operands = lax.optimization_barrier((first_parts[1], *operands))
    call = Call("second_mine", False, mine, **far)
    (second_mine,) = apply_terms(call, sizes, tables, operands)
    second_mine, first_mine = lax.optimization_barrier((second_mine, first_mine))
    out, keep = finish(True, dims, first_mine, *first_parts)
    out = finish(False, out, keep, second_mine, *second_parts)
    return out.reshape(sectors, rows, states, bond)


def solution(mesh):
    placed = (
        P("blk", None, None, None),
        P("blk", None),
        P(None, "blk"),
        P(),
        P("mpo", "blk", None, None),
        P("mpo", "blk", None, None),
        P(),
        P(),
    )
    return jax.shard_map(
        body, mesh=mesh, in_specs=placed, out_specs=P("blk", "mpo", None, None), check_vma=False
    )
```

```python
import functools

import jax
import jax.numpy as jnp
from jax import lax
from jax.experimental import pallas as pl
from jax.experimental.pallas import tpu as pltpu
from jax.sharding import PartitionSpec as P

VMEM = pl.BlockSpec(memory_space=pltpu.VMEM)
ANY = pl.BlockSpec(memory_space=pl.ANY)
PARAMS = pltpu.CompilerParams(vmem_limit_bytes=24 * 1024 * 1024)
LIGHT = pl.CostEstimate(flops=1, bytes_accessed=1, transcendentals=0)


def split(x):
    high = x.astype(jnp.bfloat16)
    low = (x - high.astype(jnp.float32)).astype(jnp.bfloat16)
    return high, low


def weighted(scales, values):
    total = scales[0] * values[0]
    for scale, value in zip(scales[1:], values[1:]):
        total = total + scale * value
    return total


def local_sector(blk, first):
    odd = lax.rem(blk, 2)
    return 1 - odd if first else odd


def partner_of(z):
    return z + 1 - 2 * lax.rem(z, 2)


def row_start(z, parity, r, groups, rows):
    dest = lax.rem(lax.div(z, 2) + r, groups) * 2 + parity
    return pl.multiple_of(dest * rows, rows)


def env_copies(first, sides, groups, rows, left_ref, right_ref, env_ref, sem, skip=0):
    z = lax.axis_index("mpo")
    some = slice(skip, skip + env_ref.shape[0])
    sector = local_sector(lax.axis_index("blk"), first)
    bond = right_ref.shape[-1]
    copies, at = [], 0
    for own in sides:
        for r in range(groups):
            start = row_start(z, lax.rem(z if own else partner_of(z), 2), r, groups, rows)
            source = left_ref.at[some, sector, pl.ds(start, rows), :]
            copies.append(pltpu.make_async_copy(source, env_ref.at[:, at : at + rows, :], sem.at[len(copies)]))
            at += rows
    source = right_ref.at[some, sector]
    copies.append(pltpu.make_async_copy(source, env_ref.at[:, at : at + bond, :], sem.at[len(copies)]))
    return copies


def front_kernel(groups, rows, states, dims_ref, theta_ref, left_ref, right_ref, *refs):
    outer_ref, inner_ref, early_ref, last_ref, dims, held, sem, early_sem, last_sem = refs
    blk = lax.axis_index("blk")
    fetches = [pltpu.make_async_copy(dims_ref, dims, sem.at[2])]
    for i, first in enumerate((False, True)):
        fetches.append(pltpu.make_async_copy(theta_ref.at[local_sector(blk, first)], held.at[i], sem.at[i]))
    copies = env_copies(False, (False,), groups, rows, left_ref, right_ref, early_ref, early_sem)
    copies += env_copies(False, (False,), groups, rows, left_ref, right_ref, last_ref, last_sem, early_ref.shape[0])
    for copy in fetches + copies:
        copy.start()
    step = 256
    fetches[0].wait()
    for i, (first, out_ref) in enumerate(((False, outer_ref), (True, inner_ref))):
        sector = local_sector(blk, first)
        fetches[i + 1].wait()

        def part(j, carry, i=i, out_ref=out_ref, sector=sector):
            start = pl.multiple_of(j * step, step)
            row = lax.broadcasted_iota(jnp.int32, (step, held.shape[2]), 0) + start
            col = lax.broadcasted_iota(jnp.int32, (step, held.shape[2]), 1)
            keep = (row < dims[sector, 0] * states) & (col < dims[sector, 1])
            out_ref[pl.ds(start, step), :] = jnp.where(keep, held[i, pl.ds(start, step), :], 0.0)
            return carry

        lax.fori_loop(0, held.shape[1] // step, part, 0)
    for copy in copies:
        copy.wait()


class Call:
    def __init__(self, name, first, cuts, slots=(), own=(), packets=(), added=False, near=None):
        self.name, self.first, self.cuts, self.slots = name, first, cuts, slots
        self.own, self.packets, self.added, self.near = own, packets, added, near
        self.leads = 0 in slots
        self.far = slots == (2,)
        self.kept = not slots


def apply_kernel(call, groups, rows, bond, site, terms, *refs):
    refs = list(refs)
    take = lambda count: [refs.pop(0) for _ in range(count)]
    table_refs = take(4)
    blocks = take(len(call.slots))
    source = take(1)[0] if call.kept else None
    left_ref, right_ref = take(2) if call.own else (None, None)
    packets = take(len(call.packets))
    before_ref = take(1)[0] if call.added else None
    outs = take(len(call.cuts))
    if call.slots:
        source = take(1)[0]
    moved, mixed, charge_ref, allowed_ref, one_ref, two_ref, sem = take(7)
    states = site * site
    z = lax.axis_index("mpo")
    sector = local_sector(lax.axis_index("blk"), call.first)
    low, high = call.cuts[0][0], call.cuts[-1][1]
    tall = high - low
    block = min(rows, 16)
    joined = 16 // block

    tables = (charge_ref, allowed_ref, one_ref, two_ref)
    copies = [pltpu.make_async_copy(a, b, sem.at[i]) for i, (a, b) in enumerate(zip(table_refs, tables))]
    sides = [(packet, partner_of(z) * terms + skip) for packet, skip in zip(packets, call.packets)]
    if call.own:
        env, env_sem = take(2)
        copies += env_copies(call.first, call.own, groups, rows, left_ref, right_ref, env, env_sem)
        sides.append((env, z * terms))
    for copy in copies:
        copy.start()

    for i, ref in enumerate(blocks):

        def part(s, carry, i=i, ref=ref):
            for u in range(0, site, 2):
                pieces = [split(ref[pl.ds(s * site + u + k, bond, stride=states), :]) for k in range(2)]
                cut = pl.ds(pl.multiple_of((s * site + u) * bond, bond), 2 * bond)
                source[i, 0:bond, cut] = jnp.concatenate([pieces[0][0], pieces[1][0]], axis=1)
                source[i, bond : 2 * bond, cut] = jnp.concatenate([pieces[0][1], pieces[1][1]], axis=1)
            return carry

        lax.fori_loop(0, site, part, 0, unroll=2)

    at = low * states
    for out in outs:
        out[...] = before_ref[at : at + out.shape[0], :] if call.added else jnp.zeros_like(out)
        at += out.shape[0]
    for copy in copies:
        copy.wait()

    def add_term(env, w, term, slot):
        left = env[w, low:high, :]
        left_rest = left - left.astype(jnp.bfloat16).astype(jnp.float32)
        stacked = jnp.concatenate([left, left_rest], axis=0).astype(jnp.bfloat16)
        rows_in = jnp.concatenate([stacked, stacked], axis=1)
        for s in range(site):
            cut = slice(s * site * bond, (s + 1) * site * bond)
            moved[:, cut] = jnp.dot(rows_in, source[slot, :, cut], preferred_element_type=jnp.float32)
        one = [[one_ref[i, j, term] for j in range(site)] for i in range(site)]
        two = [[two_ref[i, j, term] for j in range(site)] for i in range(site)]
        right = env[w, env.shape[1] - bond :, :]
        folded = jnp.concatenate(split(jnp.transpose(right)), axis=1)
        weights = jnp.concatenate([folded, folded], axis=0)
        for start in range(0, tall, block):
            half = []
            for s in range(site):
                cols = []
                for u in range(site):
                    cut = slice((s * site + u) * bond, (s * site + u + 1) * bond)
                    cols.append(moved[start : start + block, cut] + moved[tall + start : tall + start + block, cut])
                half.append([weighted(two[v], cols) for v in range(site)])
            values = [weighted(one[t], [half[s][v] for s in range(site)]) for t in range(site) for v in range(site)]
            base, size = start * states, block * states
            for p in range(0, states, joined):
                upper, lower = split(jnp.concatenate(values[p : p + joined], axis=0) if joined > 1 else values[p])
                here = base + p * block
                mixed[here : here + joined * block, 0:bond] = upper
                mixed[here : here + joined * block, bond : 2 * bond] = lower
            got = jnp.dot(mixed[base : base + size, :], weights, preferred_element_type=jnp.float32)
            got = got[:, :bond] + got[:, bond:]
            for (first_row, last_row), out in zip(call.cuts, outs):
                if first_row <= low + start < last_row:
                    at = (low + start - first_row) * states
                    out[at : at + size, :] += got

    for env, first_term in sides:

        def one_term(w, carry, env=env, first_term=first_term):
            term = first_term + w
            charge = charge_ref[term]
            shifted = sector - charge
            inside = (shifted >= 0) & (shifted <= 1)
            wanted = allowed_ref[sector, term] != 0
            if call.near is not None:
                wanted = wanted & (inside if call.near else jnp.logical_not(inside))
            if call.far:
                slot = 0
            else:
                slot = jnp.where(inside, jnp.where(charge == 0, 0 if call.first else 1, 1 if call.first else 0), 2)

            @pl.when(wanted)
            def _():
                add_term(env, w, term, slot)

            return carry

        lax.fori_loop(0, env.shape[0], one_term, 0)


def apply_terms(call, sizes, tables, operands):
    groups, rows, bond, site, terms = sizes
    states = site * site
    height = groups * rows
    tall = call.cuts[-1][1] - call.cuts[0][0]
    scratch = [
        pltpu.VMEM((2 * tall, states * bond), jnp.float32),
        pltpu.VMEM((states * tall, 2 * bond), jnp.bfloat16),
    ]
    scratch += [pltpu.SMEM(x.shape, x.dtype) for x in tables]
    scratch.append(pltpu.SemaphoreType.DMA((len(tables),)))
    places = [ANY] * 4 + [VMEM] * (len(call.slots) + call.kept)
    if call.own:
        places += [ANY, ANY]
        count = len(call.own)
        scratch.append(pltpu.VMEM((terms, count * height + bond, bond), jnp.float32))
        scratch.append(pltpu.SemaphoreType.DMA((count * groups + 1,)))
    places += [VMEM] * (len(call.packets) + call.added)
    out = [jax.ShapeDtypeStruct(((b - a) * states, bond), jnp.float32) for a, b in call.cuts]
    shape = (len(call.slots), 2 * bond, states * bond)
    if call.leads:
        out.append(jax.ShapeDtypeStruct(shape, jnp.bfloat16))
    elif call.slots:
        scratch.insert(0, pltpu.VMEM(shape, jnp.bfloat16))
    return pl.pallas_call(
        functools.partial(apply_kernel, call, *sizes),
        out_shape=tuple(out),
        in_specs=places,
        out_specs=(VMEM,) * len(out),
        scratch_shapes=scratch,
        compiler_params=PARAMS,
        cost_estimate=LIGHT,
        name=call.name,
    )(*tables, *operands)


def join_kernel(mine_ref, got_ref, out_ref):
    out_ref[...] = mine_ref[...] + got_ref[...]


def finish_kernel(first, rows, states, bond, *refs):
    if first:
        dims_ref, *parts, out_ref, keep_ref, held, sem, dims = refs
        copy = pltpu.make_async_copy(dims_ref, dims, sem.at[1])
        copy.start()
        copy.wait()
    else:
        _, keep_ref, *parts, out_ref, held, sem = refs
    blk = lax.axis_index("blk")
    sector = local_sector(blk, first)
    block = min(rows, 16)

    def mask(sector, start):
        row = lax.broadcasted_iota(jnp.int32, (block, bond), 0) + (lax.axis_index("mpo") * rows + start)
        col = lax.broadcasted_iota(jnp.int32, (block, bond), 1)
        return ((row < dims[sector, 0]) & (col < dims[sector, 1])).astype(jnp.float32)

    for start in range(0, rows, block):
        if first:
            keep = mask(sector, start)
            keep_ref[start : start + block, :] = mask(local_sector(blk, False), start)
        else:
            keep = keep_ref[start : start + block, :]
        for p in range(states):
            at = start * states + p * block
            value = parts[0][at : at + block, :]
            for other in parts[1:]:
                value = value + other[at : at + block, :]
            held[pl.ds(start * states + p, block, stride=states), :] = value * keep
    copy = pltpu.make_async_copy(held, out_ref.at[sector], sem.at[0])
    copy.start()
    copy.wait()


def body(theta, block_dims, pair_mask, term_charge, left_env, right_env, site_one, site_two):
    sectors, bond, states, _ = theta.shape
    blk_count, group_count = lax.axis_size("blk"), lax.axis_size("mpo")
    terms = left_env.shape[0]
    rows = bond // group_count
    groups = group_count // 2
    height = groups * rows
    swap = [(i, i ^ 1) for i in range(group_count)]
    flat = pltpu.with_memory_space_constraint(theta.reshape(sectors, bond * states, bond), pltpu.HBM)
    left_env = pltpu.with_memory_space_constraint(left_env, pltpu.HBM)
    right_env = pltpu.with_memory_space_constraint(right_env, pltpu.HBM)
    dims = pltpu.with_memory_space_constraint(block_dims, pltpu.HBM)

    sector_block = jax.ShapeDtypeStruct((bond * states, bond), jnp.float32)
    last = max(terms // 3, 1)
    early = terms - last
    packets = [jax.ShapeDtypeStruct((count, height + bond, bond), jnp.float32) for count in (early, last)]

    outer, inner, early_packed, last_packed = pl.pallas_call(
        functools.partial(front_kernel, groups, rows, states),
        out_shape=(sector_block, sector_block, *packets),
        in_specs=[ANY] * 4,
        out_specs=(VMEM,) * 4,
        scratch_shapes=[
            pltpu.SMEM(block_dims.shape, block_dims.dtype),
            pltpu.VMEM((2, bond * states, bond), jnp.float32),
            pltpu.SemaphoreType.DMA((3,)),
            pltpu.SemaphoreType.DMA((groups + 1,)),
            pltpu.SemaphoreType.DMA((groups + 1,)),
        ],
        compiler_params=PARAMS,
        cost_estimate=LIGHT,
        name="front",
    )(dims, flat, left_env, right_env)
    tables = (term_charge, pair_mask.T, site_one.transpose(1, 2, 0), site_two.transpose(1, 2, 0))
    pairs = blk_count // 2
    crossing = [(2 * i + 1, 2 * i + 2) for i in range(pairs - 1)]
    halo_second = lax.ppermute(outer, "blk", crossing + [(b, a) for a, b in crossing])
    halo_first = lax.ppermute(inner, "blk", [(i, i ^ 1) for i in range(2 * pairs)])
    early_env = lax.ppermute(early_packed, "mpo", swap)

    sizes = (groups, rows, bond, site_one.shape[-1], terms)
    every, mine, rest = [(0, height)], [(0, rows)], [(rows, height)]
    theirs = [(height, height + rows), (height + rows, 2 * height)]
    envs = (left_env, right_env)

    call = Call("first_own", True, mine + rest + theirs, slots=(0, 1, 2), own=(True, False))
    operands = (inner, outer, halo_first, *envs)
    first_mine, first_rest, mine_away, rest_away, source = apply_terms(call, sizes, tables, operands)
    rest_away, last_packed = lax.optimization_barrier((rest_away, last_packed))
    rest_got = lax.ppermute(rest_away, "mpo", swap)
    last_env = lax.ppermute(last_packed, "mpo", swap)
    call = Call("second_near", False, every, own=(True,), packets=(0,), near=True)
    (before,) = apply_terms(call, sizes, tables, (source, *envs, early_env))
    rest_got, before = lax.optimization_barrier((rest_got, before))
    first_rest = pl.pallas_call(
        join_kernel,
        out_shape=jax.ShapeDtypeStruct(first_rest.shape, first_rest.dtype),
        in_specs=[VMEM] * 2,
        out_specs=VMEM,
        compiler_params=PARAMS,
        cost_estimate=LIGHT,
        name="join",
    )(first_rest, rest_got)
    first_rest, before = lax.optimization_barrier((first_rest, before))
    call = Call("second_last", False, every, packets=(early,), added=True, near=True)
    (before,) = apply_terms(call, sizes, tables, (source, last_env, before))
    before, mine_away = lax.optimization_barrier((before, mine_away))
    mine_got = lax.ppermute(mine_away, "mpo", swap)
    operands = (halo_second, *envs, early_env, last_env, before)
    far = dict(slots=(2,), own=(True,), packets=(0, early), added=True, near=False)
    call = Call("second_rest", False, rest, **far)
    (second_rest,) = apply_terms(call, sizes, tables, operands)

    first_parts, second_parts = [mine_got], []
    cut = rows * states
    for r in range(1, groups):
        route = [(i, ((i // 2 + r) % groups) * 2 + i % 2) for i in range(group_count)]
        first_parts.append(lax.ppermute(first_rest[(r - 1) * cut : r * cut], "mpo", route))
        second_parts.append(lax.ppermute(second_rest[(r - 1) * cut : r * cut], "mpo", route))

    def finish(first, *operands):
        out = jax.ShapeDtypeStruct((sectors, rows * states, bond), jnp.float32)
        keep = jax.ShapeDtypeStruct((rows, bond), jnp.float32)
        scratch = [pltpu.VMEM((rows * states, bond), jnp.float32), pltpu.SemaphoreType.DMA((2,))]
        if first:
            scratch.append(pltpu.SMEM(block_dims.shape, block_dims.dtype))
        return pl.pallas_call(
            functools.partial(finish_kernel, first, rows, states, bond),
            out_shape=(out, keep) if first else out,
            in_specs=[ANY] + [VMEM] * (len(operands) - 1),
            out_specs=(ANY, VMEM) if first else ANY,
            scratch_shapes=scratch,
            input_output_aliases={} if first else {0: 0},
            compiler_params=PARAMS,
            cost_estimate=LIGHT,
            name="finish_first" if first else "finish_second",
        )(*operands)

    first_parts[1], *operands = lax.optimization_barrier((first_parts[1], *operands))
    call = Call("second_mine", False, mine, **far)
    (second_mine,) = apply_terms(call, sizes, tables, operands)
    second_mine, first_mine = lax.optimization_barrier((second_mine, first_mine))
    out, keep = finish(True, dims, first_mine, *first_parts)
    out = finish(False, out, keep, second_mine, *second_parts)
    return out.reshape(sectors, rows, states, bond)


def solution(mesh):
    placed = (
        P("blk", None, None, None),
        P("blk", None),
        P(None, "blk"),
        P(),
        P("mpo", "blk", None, None),
        P("mpo", "blk", None, None),
        P(),
        P(),
    )
    return jax.shard_map(
        body, mesh=mesh, in_specs=placed, out_specs=P("blk", "mpo", None, None), check_vma=False
    )
```

```python
import functools

import jax
import jax.numpy as jnp
from jax import lax
from jax.experimental import pallas as pl
from jax.experimental.pallas import tpu as pltpu
from jax.sharding import PartitionSpec as P

VMEM = pl.BlockSpec(memory_space=pltpu.VMEM)
ANY = pl.BlockSpec(memory_space=pl.ANY)
PARAMS = pltpu.CompilerParams(vmem_limit_bytes=24 * 1024 * 1024)
LIGHT = pl.CostEstimate(flops=1, bytes_accessed=1, transcendentals=0)


def split(x):
    high = x.astype(jnp.bfloat16)
    low = (x - high.astype(jnp.float32)).astype(jnp.bfloat16)
    return high, low


def weighted(scales, values):
    total = scales[0] * values[0]
    for scale, value in zip(scales[1:], values[1:]):
        total = total + scale * value
    return total


def local_sector(blk, first):
    odd = lax.rem(blk, 2)
    return 1 - odd if first else odd


def partner_of(z):
    return z + 1 - 2 * lax.rem(z, 2)


def row_start(z, parity, r, groups, rows):
    dest = lax.rem(lax.div(z, 2) + r, groups) * 2 + parity
    return pl.multiple_of(dest * rows, rows)


def env_copies(first, sides, groups, rows, left_ref, right_ref, env_ref, sem, skip=0):
    z = lax.axis_index("mpo")
    some = slice(skip, skip + env_ref.shape[0])
    sector = local_sector(lax.axis_index("blk"), first)
    bond = right_ref.shape[-1]
    copies, at = [], 0
    for own in sides:
        for r in range(groups):
            start = row_start(z, lax.rem(z if own else partner_of(z), 2), r, groups, rows)
            source = left_ref.at[some, sector, pl.ds(start, rows), :]
            copies.append(pltpu.make_async_copy(source, env_ref.at[:, at : at + rows, :], sem.at[len(copies)]))
            at += rows
    source = right_ref.at[some, sector]
    copies.append(pltpu.make_async_copy(source, env_ref.at[:, at : at + bond, :], sem.at[len(copies)]))
    return copies


def front_kernel(groups, rows, states, dims_ref, theta_ref, left_ref, right_ref, *refs):
    outer_ref, inner_ref, early_ref, last_ref, dims, held, sem, early_sem, last_sem = refs
    blk = lax.axis_index("blk")
    fetches = [pltpu.make_async_copy(dims_ref, dims, sem.at[2])]
    for i, first in enumerate((False, True)):
        fetches.append(pltpu.make_async_copy(theta_ref.at[local_sector(blk, first)], held.at[i], sem.at[i]))
    copies = env_copies(False, (False,), groups, rows, left_ref, right_ref, early_ref, early_sem)
    copies += env_copies(False, (False,), groups, rows, left_ref, right_ref, last_ref, last_sem, early_ref.shape[0])
    for copy in fetches + copies:
        copy.start()
    step = 256
    fetches[0].wait()
    for i, (first, out_ref) in enumerate(((False, outer_ref), (True, inner_ref))):
        sector = local_sector(blk, first)
        fetches[i + 1].wait()

        def part(j, carry, i=i, out_ref=out_ref, sector=sector):
            start = pl.multiple_of(j * step, step)
            row = lax.broadcasted_iota(jnp.int32, (step, held.shape[2]), 0) + start
            col = lax.broadcasted_iota(jnp.int32, (step, held.shape[2]), 1)
            keep = (row < dims[sector, 0] * states) & (col < dims[sector, 1])
            out_ref[pl.ds(start, step), :] = jnp.where(keep, held[i, pl.ds(start, step), :], 0.0)
            return carry

        lax.fori_loop(0, held.shape[1] // step, part, 0)
    for copy in copies:
        copy.wait()


class Call:
    def __init__(self, name, first, cuts, slots=(), own=(), packets=(), added=False, near=None, whole=()):
        self.name, self.first, self.cuts, self.slots = name, first, cuts, slots
        self.own, self.packets, self.added, self.near = own, packets, added, near
        self.leads = 0 in slots
        self.far = slots == (2,)
        self.whole = whole
        self.kept = not slots or bool(whole)


def apply_kernel(call, groups, rows, bond, site, terms, *refs):
    refs = list(refs)
    take = lambda count: [refs.pop(0) for _ in range(count)]
    table_refs = take(4)
    blocks = take(len(call.slots))
    kept = source = take(1)[0] if call.kept else None
    left_ref, right_ref = take(2) if call.own else (None, None)
    packets = take(len(call.packets))
    before_ref = take(1)[0] if call.added else None
    outs = take(len(call.cuts))
    if call.slots:
        source = take(1)[0]
    moved, mixed, charge_ref, allowed_ref, one_ref, two_ref, sem = take(7)
    states = site * site
    z = lax.axis_index("mpo")
    sector = local_sector(lax.axis_index("blk"), call.first)
    low, high = call.cuts[0][0], call.cuts[-1][1]
    tall = high - low
    block = min(rows, 16)
    joined = 16 // block

    tables = (charge_ref, allowed_ref, one_ref, two_ref)
    copies = [pltpu.make_async_copy(a, b, sem.at[i]) for i, (a, b) in enumerate(zip(table_refs, tables))]
    sides = [(packet, partner_of(z) * terms + skip, call.near) for packet, skip in zip(packets, call.packets)]
    sides += [(packets[i], partner_of(z) * terms + call.packets[i], True) for i in call.whole]
    if call.own:
        env, env_sem = take(2)
        copies += env_copies(call.first, call.own, groups, rows, left_ref, right_ref, env, env_sem)
        sides.append((env, z * terms, call.near))
    for copy in copies:
        copy.start()

    for i, ref in enumerate(blocks):

        def part(s, carry, i=i, ref=ref):
            for u in range(0, site, 2):
                pieces = [split(ref[pl.ds(s * site + u + k, bond, stride=states), :]) for k in range(2)]
                cut = pl.ds(pl.multiple_of((s * site + u) * bond, bond), 2 * bond)
                source[i, 0:bond, cut] = jnp.concatenate([pieces[0][0], pieces[1][0]], axis=1)
                source[i, bond : 2 * bond, cut] = jnp.concatenate([pieces[0][1], pieces[1][1]], axis=1)
            return carry

        lax.fori_loop(0, site, part, 0, unroll=2)

    at = low * states
    for out in outs:
        out[...] = before_ref[at : at + out.shape[0], :] if call.added else jnp.zeros_like(out)
        at += out.shape[0]
    for copy in copies:
        copy.wait()

    def add_term(env, w, term, source, slot):
        left = env[w, low:high, :]
        left_rest = left - left.astype(jnp.bfloat16).astype(jnp.float32)
        stacked = jnp.concatenate([left, left_rest], axis=0).astype(jnp.bfloat16)
        rows_in = jnp.concatenate([stacked, stacked], axis=1)
        for s in range(site):
            cut = slice(s * site * bond, (s + 1) * site * bond)
            moved[:, cut] = jnp.dot(rows_in, source[slot, :, cut], preferred_element_type=jnp.float32)
        one = [[one_ref[i, j, term] for j in range(site)] for i in range(site)]
        two = [[two_ref[i, j, term] for j in range(site)] for i in range(site)]
        right = env[w, env.shape[1] - bond :, :]
        folded = jnp.concatenate(split(jnp.transpose(right)), axis=1)
        weights = jnp.concatenate([folded, folded], axis=0)
        for start in range(0, tall, block):
            half = []
            for s in range(site):
                cols = []
                for u in range(site):
                    cut = slice((s * site + u) * bond, (s * site + u + 1) * bond)
                    cols.append(moved[start : start + block, cut] + moved[tall + start : tall + start + block, cut])
                half.append([weighted(two[v], cols) for v in range(site)])
            values = [weighted(one[t], [half[s][v] for s in range(site)]) for t in range(site) for v in range(site)]
            base, size = start * states, block * states
            for p in range(0, states, joined):
                upper, lower = split(jnp.concatenate(values[p : p + joined], axis=0) if joined > 1 else values[p])
                here = base + p * block
                mixed[here : here + joined * block, 0:bond] = upper
                mixed[here : here + joined * block, bond : 2 * bond] = lower
            got = jnp.dot(mixed[base : base + size, :], weights, preferred_element_type=jnp.float32)
            got = got[:, :bond] + got[:, bond:]
            for (first_row, last_row), out in zip(call.cuts, outs):
                if first_row <= low + start < last_row:
                    at = (low + start - first_row) * states
                    out[at : at + size, :] += got

    for env, first_term, near in sides:

        def one_term(w, carry, env=env, first_term=first_term, near=near):
            term = first_term + w
            charge = charge_ref[term]
            shifted = sector - charge
            inside = (shifted >= 0) & (shifted <= 1)
            wanted = allowed_ref[sector, term] != 0
            if near is not None:
                wanted = wanted & (inside if near else jnp.logical_not(inside))
            chosen = source
            if call.far and not near:
                slot = 0
            else:
                chosen = kept if call.kept else source
                slot = jnp.where(inside, jnp.where(charge == 0, 0 if call.first else 1, 1 if call.first else 0), 2)

            @pl.when(wanted)
            def _():
                add_term(env, w, term, chosen, slot)

            return carry

        lax.fori_loop(0, env.shape[0], one_term, 0)


def apply_terms(call, sizes, tables, operands):
    groups, rows, bond, site, terms = sizes
    states = site * site
    height = groups * rows
    tall = call.cuts[-1][1] - call.cuts[0][0]
    scratch = [
        pltpu.VMEM((2 * tall, states * bond), jnp.float32),
        pltpu.VMEM((states * tall, 2 * bond), jnp.bfloat16),
    ]
    scratch += [pltpu.SMEM(x.shape, x.dtype) for x in tables]
    scratch.append(pltpu.SemaphoreType.DMA((len(tables),)))
    places = [ANY] * 4 + [VMEM] * (len(call.slots) + call.kept)
    if call.own:
        places += [ANY, ANY]
        count = len(call.own)
        scratch.append(pltpu.VMEM((terms, count * height + bond, bond), jnp.float32))
        scratch.append(pltpu.SemaphoreType.DMA((count * groups + 1,)))
    places += [VMEM] * (len(call.packets) + call.added)
    out = [jax.ShapeDtypeStruct(((b - a) * states, bond), jnp.float32) for a, b in call.cuts]
    shape = (len(call.slots), 2 * bond, states * bond)
    if call.leads:
        out.append(jax.ShapeDtypeStruct(shape, jnp.bfloat16))
    elif call.slots:
        scratch.insert(0, pltpu.VMEM(shape, jnp.bfloat16))
    return pl.pallas_call(
        functools.partial(apply_kernel, call, *sizes),
        out_shape=tuple(out),
        in_specs=places,
        out_specs=(VMEM,) * len(out),
        scratch_shapes=scratch,
        compiler_params=PARAMS,
        cost_estimate=LIGHT,
        name=call.name,
    )(*tables, *operands)


def join_kernel(mine_ref, got_ref, out_ref):
    out_ref[...] = mine_ref[...] + got_ref[...]


def finish_kernel(first, rows, states, bond, *refs):
    if first:
        dims_ref, *parts, out_ref, keep_ref, held, sem, dims = refs
        copy = pltpu.make_async_copy(dims_ref, dims, sem.at[1])
        copy.start()
        copy.wait()
    else:
        _, keep_ref, *parts, out_ref, held, sem = refs
    blk = lax.axis_index("blk")
    sector = local_sector(blk, first)
    block = min(rows, 16)

    def mask(sector, start):
        row = lax.broadcasted_iota(jnp.int32, (block, bond), 0) + (lax.axis_index("mpo") * rows + start)
        col = lax.broadcasted_iota(jnp.int32, (block, bond), 1)
        return ((row < dims[sector, 0]) & (col < dims[sector, 1])).astype(jnp.float32)

    for start in range(0, rows, block):
        if first:
            keep = mask(sector, start)
            keep_ref[start : start + block, :] = mask(local_sector(blk, False), start)
        else:
            keep = keep_ref[start : start + block, :]
        for p in range(states):
            at = start * states + p * block
            value = parts[0][at : at + block, :]
            for other in parts[1:]:
                value = value + other[at : at + block, :]
            held[pl.ds(start * states + p, block, stride=states), :] = value * keep
    copy = pltpu.make_async_copy(held, out_ref.at[sector], sem.at[0])
    copy.start()
    copy.wait()


def body(theta, block_dims, pair_mask, term_charge, left_env, right_env, site_one, site_two):
    sectors, bond, states, _ = theta.shape
    blk_count, group_count = lax.axis_size("blk"), lax.axis_size("mpo")
    terms = left_env.shape[0]
    rows = bond // group_count
    groups = group_count // 2
    height = groups * rows
    swap = [(i, i ^ 1) for i in range(group_count)]
    flat = pltpu.with_memory_space_constraint(theta.reshape(sectors, bond * states, bond), pltpu.HBM)
    left_env = pltpu.with_memory_space_constraint(left_env, pltpu.HBM)
    right_env = pltpu.with_memory_space_constraint(right_env, pltpu.HBM)
    dims = pltpu.with_memory_space_constraint(block_dims, pltpu.HBM)

    sector_block = jax.ShapeDtypeStruct((bond * states, bond), jnp.float32)
    last = max(terms // 3, 1)
    early = terms - last
    packets = [jax.ShapeDtypeStruct((count, height + bond, bond), jnp.float32) for count in (early, last)]

    outer, inner, early_packed, last_packed = pl.pallas_call(
        functools.partial(front_kernel, groups, rows, states),
        out_shape=(sector_block, sector_block, *packets),
        in_specs=[ANY] * 4,
        out_specs=(VMEM,) * 4,
        scratch_shapes=[
            pltpu.SMEM(block_dims.shape, block_dims.dtype),
            pltpu.VMEM((2, bond * states, bond), jnp.float32),
            pltpu.SemaphoreType.DMA((3,)),
            pltpu.SemaphoreType.DMA((groups + 1,)),
            pltpu.SemaphoreType.DMA((groups + 1,)),
        ],
        compiler_params=PARAMS,
        cost_estimate=LIGHT,
        name="front",
    )(dims, flat, left_env, right_env)
    tables = (term_charge, pair_mask.T, site_one.transpose(1, 2, 0), site_two.transpose(1, 2, 0))
    pairs = blk_count // 2
    crossing = [(2 * i + 1, 2 * i + 2) for i in range(pairs - 1)]
    halo_second = lax.ppermute(outer, "blk", crossing + [(b, a) for a, b in crossing])
    halo_first = lax.ppermute(inner, "blk", [(i, i ^ 1) for i in range(2 * pairs)])
    early_env = lax.ppermute(early_packed, "mpo", swap)

    sizes = (groups, rows, bond, site_one.shape[-1], terms)
    every, mine, rest = [(0, height)], [(0, rows)], [(rows, height)]
    theirs = [(height, height + rows), (height + rows, 2 * height)]
    envs = (left_env, right_env)

    call = Call("first_own", True, mine + rest + theirs, slots=(0, 1, 2), own=(True, False))
    operands = (inner, outer, halo_first, *envs)
    first_mine, first_rest, mine_away, rest_away, source = apply_terms(call, sizes, tables, operands)
    rest_away, last_packed = lax.optimization_barrier((rest_away, last_packed))
    rest_got = lax.ppermute(rest_away, "mpo", swap)
    last_env = lax.ppermute(last_packed, "mpo", swap)
    call = Call("second_near", False, every, own=(True,), packets=(0,), near=True)
    (before,) = apply_terms(call, sizes, tables, (source, *envs, early_env))
    rest_got, before = lax.optimization_barrier((rest_got, before))
    first_rest = pl.pallas_call(
        join_kernel,
        out_shape=jax.ShapeDtypeStruct(first_rest.shape, first_rest.dtype),
        in_specs=[VMEM] * 2,
        out_specs=VMEM,
        compiler_params=PARAMS,
        cost_estimate=LIGHT,
        name="join",
    )(first_rest, rest_got)
    first_rest, before = lax.optimization_barrier((first_rest, before))
    last_env, mine_away = lax.optimization_barrier((last_env, mine_away))
    mine_got = lax.ppermute(mine_away, "mpo", swap)
    operands = (halo_second, source, *envs, early_env, last_env, before)
    far = dict(slots=(2,), own=(True,), packets=(0, early), added=True, near=False, whole=(1,))
    call = Call("second_rest", False, rest, **far)
    (second_rest,) = apply_terms(call, sizes, tables, operands)

    first_parts, second_parts = [mine_got], []
    cut = rows * states
    for r in range(1, groups):
        route = [(i, ((i // 2 + r) % groups) * 2 + i % 2) for i in range(group_count)]
        first_parts.append(lax.ppermute(first_rest[(r - 1) * cut : r * cut], "mpo", route))
        second_parts.append(lax.ppermute(second_rest[(r - 1) * cut : r * cut], "mpo", route))

    def finish(first, *operands):
        out = jax.ShapeDtypeStruct((sectors, rows * states, bond), jnp.float32)
        keep = jax.ShapeDtypeStruct((rows, bond), jnp.float32)
        scratch = [pltpu.VMEM((rows * states, bond), jnp.float32), pltpu.SemaphoreType.DMA((2,))]
        if first:
            scratch.append(pltpu.SMEM(block_dims.shape, block_dims.dtype))
        return pl.pallas_call(
            functools.partial(finish_kernel, first, rows, states, bond),
            out_shape=(out, keep) if first else out,
            in_specs=[ANY] + [VMEM] * (len(operands) - 1),
            out_specs=(ANY, VMEM) if first else ANY,
            scratch_shapes=scratch,
            input_output_aliases={} if first else {0: 0},
            compiler_params=PARAMS,
            cost_estimate=LIGHT,
            name="finish_first" if first else "finish_second",
        )(*operands)

    first_parts[1], *operands = lax.optimization_barrier((first_parts[1], *operands))
    call = Call("second_mine", False, mine, **far)
    (second_mine,) = apply_terms(call, sizes, tables, operands)
    second_mine, first_mine = lax.optimization_barrier((second_mine, first_mine))
    out, keep = finish(True, dims, first_mine, *first_parts)
    out = finish(False, out, keep, second_mine, *second_parts)
    return out.reshape(sectors, rows, states, bond)


def solution(mesh):
    placed = (
        P("blk", None, None, None),
        P("blk", None),
        P(None, "blk"),
        P(),
        P("mpo", "blk", None, None),
        P("mpo", "blk", None, None),
        P(),
        P(),
    )
    return jax.shard_map(
        body, mesh=mesh, in_specs=placed, out_specs=P("blk", "mpo", None, None), check_vma=False
    )
```

```python
import functools

import jax
import jax.numpy as jnp
from jax import lax
from jax.experimental import pallas as pl
from jax.experimental.pallas import tpu as pltpu
from jax.sharding import PartitionSpec as P

VMEM = pl.BlockSpec(memory_space=pltpu.VMEM)
ANY = pl.BlockSpec(memory_space=pl.ANY)
PARAMS = pltpu.CompilerParams(vmem_limit_bytes=24 * 1024 * 1024)
LIGHT = pl.CostEstimate(flops=1, bytes_accessed=1, transcendentals=0)


def split(x):
    high = x.astype(jnp.bfloat16)
    low = (x - high.astype(jnp.float32)).astype(jnp.bfloat16)
    return high, low


def weighted(scales, values):
    total = scales[0] * values[0]
    for scale, value in zip(scales[1:], values[1:]):
        total = total + scale * value
    return total


def local_sector(blk, first):
    odd = lax.rem(blk, 2)
    return 1 - odd if first else odd


def partner_of(z):
    return z + 1 - 2 * lax.rem(z, 2)


def row_start(z, parity, r, groups, rows):
    dest = lax.rem(lax.div(z, 2) + r, groups) * 2 + parity
    return pl.multiple_of(dest * rows, rows)


def env_copies(first, sides, groups, rows, left_ref, right_ref, env_ref, sem, skip=0):
    z = lax.axis_index("mpo")
    some = slice(skip, skip + env_ref.shape[0])
    sector = local_sector(lax.axis_index("blk"), first)
    bond = right_ref.shape[-1]
    copies, at = [], 0
    for own in sides:
        for r in range(groups):
            start = row_start(z, lax.rem(z if own else partner_of(z), 2), r, groups, rows)
            source = left_ref.at[some, sector, pl.ds(start, rows), :]
            copies.append(pltpu.make_async_copy(source, env_ref.at[:, at : at + rows, :], sem.at[len(copies)]))
            at += rows
    source = right_ref.at[some, sector]
    copies.append(pltpu.make_async_copy(source, env_ref.at[:, at : at + bond, :], sem.at[len(copies)]))
    return copies


def front_kernel(groups, rows, states, dims_ref, theta_ref, left_ref, right_ref, *refs):
    outer_ref, inner_ref, early_ref, last_ref, dims, held, sem, early_sem, last_sem = refs
    blk = lax.axis_index("blk")
    fetches = [pltpu.make_async_copy(dims_ref, dims, sem.at[2])]
    for i, first in enumerate((False, True)):
        fetches.append(pltpu.make_async_copy(theta_ref.at[local_sector(blk, first)], held.at[i], sem.at[i]))
    copies = env_copies(False, (False,), groups, rows, left_ref, right_ref, early_ref, early_sem)
    copies += env_copies(False, (False,), groups, rows, left_ref, right_ref, last_ref, last_sem, early_ref.shape[0])
    for copy in fetches + copies:
        copy.start()
    step = 256
    fetches[0].wait()
    for i, (first, out_ref) in enumerate(((False, outer_ref), (True, inner_ref))):
        sector = local_sector(blk, first)
        fetches[i + 1].wait()

        def part(j, carry, i=i, out_ref=out_ref, sector=sector):
            start = pl.multiple_of(j * step, step)
            row = lax.broadcasted_iota(jnp.int32, (step, held.shape[2]), 0) + start
            col = lax.broadcasted_iota(jnp.int32, (step, held.shape[2]), 1)
            keep = (row < dims[sector, 0] * states) & (col < dims[sector, 1])
            out_ref[pl.ds(start, step), :] = jnp.where(keep, held[i, pl.ds(start, step), :], 0.0)
            return carry

        lax.fori_loop(0, held.shape[1] // step, part, 0)
    for copy in copies:
        copy.wait()


class Call:
    def __init__(self, name, first, cuts, slots=(), own=(), packets=(), added=False, near=None, whole=()):
        self.name, self.first, self.cuts, self.slots = name, first, cuts, slots
        self.own, self.packets, self.added, self.near = own, packets, added, near
        self.leads = 0 in slots
        self.far = slots == (2,)
        self.whole = whole
        self.kept = not slots or bool(whole)


def apply_kernel(call, groups, rows, bond, site, terms, *refs):
    refs = list(refs)
    take = lambda count: [refs.pop(0) for _ in range(count)]
    table_refs = take(4)
    blocks = take(len(call.slots))
    kept = source = take(1)[0] if call.kept else None
    left_ref, right_ref = take(2) if call.own else (None, None)
    packets = take(len(call.packets))
    before_ref = take(1)[0] if call.added else None
    outs = take(len(call.cuts))
    if call.slots:
        source = take(1)[0]
    moved, mixed, charge_ref, allowed_ref, one_ref, two_ref, sem = take(7)
    states = site * site
    z = lax.axis_index("mpo")
    sector = local_sector(lax.axis_index("blk"), call.first)
    low, high = call.cuts[0][0], call.cuts[-1][1]
    tall = high - low
    block = min(rows, 16)
    joined = 16 // block

    tables = (charge_ref, allowed_ref, one_ref, two_ref)
    copies = [pltpu.make_async_copy(a, b, sem.at[i]) for i, (a, b) in enumerate(zip(table_refs, tables))]
    sides = [(packet, partner_of(z) * terms + skip, call.near) for packet, skip in zip(packets, call.packets)]
    sides += [(packets[i], partner_of(z) * terms + call.packets[i], True) for i in call.whole]
    if call.own:
        env, env_sem = take(2)
        copies += env_copies(call.first, call.own, groups, rows, left_ref, right_ref, env, env_sem)
        sides.append((env, z * terms, call.near))
    late = copies[len(tables) :]
    copies = copies[: len(tables)]
    for copy in copies + late:
        copy.start()

    for i, ref in enumerate(blocks):

        def part(s, carry, i=i, ref=ref):
            for u in range(0, site, 2):
                pieces = [split(ref[pl.ds(s * site + u + k, bond, stride=states), :]) for k in range(2)]
                cut = pl.ds(pl.multiple_of((s * site + u) * bond, bond), 2 * bond)
                source[i, 0:bond, cut] = jnp.concatenate([pieces[0][0], pieces[1][0]], axis=1)
                source[i, bond : 2 * bond, cut] = jnp.concatenate([pieces[0][1], pieces[1][1]], axis=1)
            return carry

        lax.fori_loop(0, site, part, 0, unroll=2)

    at = low * states
    for out in outs:
        out[...] = before_ref[at : at + out.shape[0], :] if call.added else jnp.zeros_like(out)
        at += out.shape[0]
    for copy in copies:
        copy.wait()

    def add_term(env, w, term, source, slot):
        left = env[w, low:high, :]
        left_rest = left - left.astype(jnp.bfloat16).astype(jnp.float32)
        stacked = jnp.concatenate([left, left_rest], axis=0).astype(jnp.bfloat16)
        rows_in = jnp.concatenate([stacked, stacked], axis=1)
        for s in range(site):
            cut = slice(s * site * bond, (s + 1) * site * bond)
            moved[:, cut] = jnp.dot(rows_in, source[slot, :, cut], preferred_element_type=jnp.float32)
        one = [[one_ref[i, j, term] for j in range(site)] for i in range(site)]
        two = [[two_ref[i, j, term] for j in range(site)] for i in range(site)]
        right = env[w, env.shape[1] - bond :, :]
        folded = jnp.concatenate(split(jnp.transpose(right)), axis=1)
        weights = jnp.concatenate([folded, folded], axis=0)
        for start in range(0, tall, block):
            half = []
            for s in range(site):
                cols = []
                for u in range(site):
                    cut = slice((s * site + u) * bond, (s * site + u + 1) * bond)
                    cols.append(moved[start : start + block, cut] + moved[tall + start : tall + start + block, cut])
                half.append([weighted(two[v], cols) for v in range(site)])
            values = [weighted(one[t], [half[s][v] for s in range(site)]) for t in range(site) for v in range(site)]
            base, size = start * states, block * states
            for p in range(0, states, joined):
                upper, lower = split(jnp.concatenate(values[p : p + joined], axis=0) if joined > 1 else values[p])
                here = base + p * block
                mixed[here : here + joined * block, 0:bond] = upper
                mixed[here : here + joined * block, bond : 2 * bond] = lower
            got = jnp.dot(mixed[base : base + size, :], weights, preferred_element_type=jnp.float32)
            got = got[:, :bond] + got[:, bond:]
            for (first_row, last_row), out in zip(call.cuts, outs):
                if first_row <= low + start < last_row:
                    at = (low + start - first_row) * states
                    out[at : at + size, :] += got

    for n, (env, first_term, near) in enumerate(sides):
        if n == len(sides) - 1:
            for copy in late:
                copy.wait()

        def one_term(w, carry, env=env, first_term=first_term, near=near):
            term = first_term + w
            charge = charge_ref[term]
            shifted = sector - charge
            inside = (shifted >= 0) & (shifted <= 1)
            wanted = allowed_ref[sector, term] != 0
            if near is not None:
                wanted = wanted & (inside if near else jnp.logical_not(inside))
            chosen = source
            if call.far and not near:
                slot = 0
            else:
                chosen = kept if call.kept else source
                slot = jnp.where(inside, jnp.where(charge == 0, 0 if call.first else 1, 1 if call.first else 0), 2)

            @pl.when(wanted)
            def _():
                add_term(env, w, term, chosen, slot)

            return carry

        lax.fori_loop(0, env.shape[0], one_term, 0)


def apply_terms(call, sizes, tables, operands):
    groups, rows, bond, site, terms = sizes
    states = site * site
    height = groups * rows
    tall = call.cuts[-1][1] - call.cuts[0][0]
    scratch = [
        pltpu.VMEM((2 * tall, states * bond), jnp.float32),
        pltpu.VMEM((states * tall, 2 * bond), jnp.bfloat16),
    ]
    scratch += [pltpu.SMEM(x.shape, x.dtype) for x in tables]
    scratch.append(pltpu.SemaphoreType.DMA((len(tables),)))
    places = [ANY] * 4 + [VMEM] * (len(call.slots) + call.kept)
    if call.own:
        places += [ANY, ANY]
        count = len(call.own)
        scratch.append(pltpu.VMEM((terms, count * height + bond, bond), jnp.float32))
        scratch.append(pltpu.SemaphoreType.DMA((count * groups + 1,)))
    places += [VMEM] * (len(call.packets) + call.added)
    out = [jax.ShapeDtypeStruct(((b - a) * states, bond), jnp.float32) for a, b in call.cuts]
    shape = (len(call.slots), 2 * bond, states * bond)
    if call.leads:
        out.append(jax.ShapeDtypeStruct(shape, jnp.bfloat16))
    elif call.slots:
        scratch.insert(0, pltpu.VMEM(shape, jnp.bfloat16))
    return pl.pallas_call(
        functools.partial(apply_kernel, call, *sizes),
        out_shape=tuple(out),
        in_specs=places,
        out_specs=(VMEM,) * len(out),
        scratch_shapes=scratch,
        compiler_params=PARAMS,
        cost_estimate=LIGHT,
        name=call.name,
    )(*tables, *operands)


def join_kernel(mine_ref, got_ref, out_ref):
    out_ref[...] = mine_ref[...] + got_ref[...]


def finish_kernel(first, rows, states, bond, *refs):
    if first:
        dims_ref, *parts, out_ref, keep_ref, held, sem, dims = refs
        copy = pltpu.make_async_copy(dims_ref, dims, sem.at[1])
        copy.start()
        copy.wait()
    else:
        _, keep_ref, *parts, out_ref, held, sem = refs
    blk = lax.axis_index("blk")
    sector = local_sector(blk, first)
    block = min(rows, 16)

    def mask(sector, start):
        row = lax.broadcasted_iota(jnp.int32, (block, bond), 0) + (lax.axis_index("mpo") * rows + start)
        col = lax.broadcasted_iota(jnp.int32, (block, bond), 1)
        return ((row < dims[sector, 0]) & (col < dims[sector, 1])).astype(jnp.float32)

    copies = []
    for start in range(0, rows, block):
        if first:
            keep = mask(sector, start)
            keep_ref[start : start + block, :] = mask(local_sector(blk, False), start)
        else:
            keep = keep_ref[start : start + block, :]
        for p in range(states):
            at = start * states + p * block
            value = parts[0][at : at + block, :]
            for other in parts[1:]:
                value = value + other[at : at + block, :]
            held[pl.ds(start * states + p, block, stride=states), :] = value * keep
        some = pl.ds(start * states, block * states)
        copies.append(pltpu.make_async_copy(held.at[some, :], out_ref.at[sector, some, :], sem.at[2 + len(copies)]))
        copies[-1].start()
    for copy in copies:
        copy.wait()


def body(theta, block_dims, pair_mask, term_charge, left_env, right_env, site_one, site_two):
    sectors, bond, states, _ = theta.shape
    blk_count, group_count = lax.axis_size("blk"), lax.axis_size("mpo")
    terms = left_env.shape[0]
    rows = bond // group_count
    groups = group_count // 2
    height = groups * rows
    swap = [(i, i ^ 1) for i in range(group_count)]
    flat = pltpu.with_memory_space_constraint(theta.reshape(sectors, bond * states, bond), pltpu.HBM)
    left_env = pltpu.with_memory_space_constraint(left_env, pltpu.HBM)
    right_env = pltpu.with_memory_space_constraint(right_env, pltpu.HBM)
    dims = pltpu.with_memory_space_constraint(block_dims, pltpu.HBM)

    sector_block = jax.ShapeDtypeStruct((bond * states, bond), jnp.float32)
    last = max(terms // 3, 1)
    early = terms - last
    packets = [jax.ShapeDtypeStruct((count, height + bond, bond), jnp.float32) for count in (early, last)]

    outer, inner, early_packed, last_packed = pl.pallas_call(
        functools.partial(front_kernel, groups, rows, states),
        out_shape=(sector_block, sector_block, *packets),
        in_specs=[ANY] * 4,
        out_specs=(VMEM,) * 4,
        scratch_shapes=[
            pltpu.SMEM(block_dims.shape, block_dims.dtype),
            pltpu.VMEM((2, bond * states, bond), jnp.float32),
            pltpu.SemaphoreType.DMA((3,)),
            pltpu.SemaphoreType.DMA((groups + 1,)),
            pltpu.SemaphoreType.DMA((groups + 1,)),
        ],
        compiler_params=PARAMS,
        cost_estimate=LIGHT,
        name="front",
    )(dims, flat, left_env, right_env)
    tables = (term_charge, pair_mask.T, site_one.transpose(1, 2, 0), site_two.transpose(1, 2, 0))
    pairs = blk_count // 2
    crossing = [(2 * i + 1, 2 * i + 2) for i in range(pairs - 1)]
    halo_second = lax.ppermute(outer, "blk", crossing + [(b, a) for a, b in crossing])
    halo_first = lax.ppermute(inner, "blk", [(i, i ^ 1) for i in range(2 * pairs)])
    early_env = lax.ppermute(early_packed, "mpo", swap)

    sizes = (groups, rows, bond, site_one.shape[-1], terms)
    every, mine, rest = [(0, height)], [(0, rows)], [(rows, height)]
    theirs = [(height, height + rows), (height + rows, 2 * height)]
    envs = (left_env, right_env)

    call = Call("first_own", True, mine + rest + theirs, slots=(0, 1, 2), own=(True, False))
    operands = (inner, outer, halo_first, *envs)
    first_mine, first_rest, mine_away, rest_away, source = apply_terms(call, sizes, tables, operands)
    rest_away, last_packed = lax.optimization_barrier((rest_away, last_packed))
    rest_got = lax.ppermute(rest_away, "mpo", swap)
    last_env = lax.ppermute(last_packed, "mpo", swap)
    call = Call("second_near", False, every, own=(True,), packets=(0,), near=True)
    (before,) = apply_terms(call, sizes, tables, (source, *envs, early_env))
    rest_got, before = lax.optimization_barrier((rest_got, before))
    first_rest = pl.pallas_call(
        join_kernel,
        out_shape=jax.ShapeDtypeStruct(first_rest.shape, first_rest.dtype),
        in_specs=[VMEM] * 2,
        out_specs=VMEM,
        compiler_params=PARAMS,
        cost_estimate=LIGHT,
        name="join",
    )(first_rest, rest_got)
    first_rest, before = lax.optimization_barrier((first_rest, before))
    last_env, mine_away = lax.optimization_barrier((last_env, mine_away))
    mine_got = lax.ppermute(mine_away, "mpo", swap)
    operands = (halo_second, source, *envs, early_env, last_env, before)
    far = dict(slots=(2,), own=(True,), packets=(0, early), added=True, near=False, whole=(1,))
    call = Call("second_rest", False, rest, **far)
    (second_rest,) = apply_terms(call, sizes, tables, operands)

    first_parts, second_parts = [mine_got], []
    cut = rows * states
    for r in range(1, groups):
        route = [(i, ((i // 2 + r) % groups) * 2 + i % 2) for i in range(group_count)]
        first_parts.append(lax.ppermute(first_rest[(r - 1) * cut : r * cut], "mpo", route))
        second_parts.append(lax.ppermute(second_rest[(r - 1) * cut : r * cut], "mpo", route))

    def finish(first, *operands):
        out = jax.ShapeDtypeStruct((sectors, rows * states, bond), jnp.float32)
        keep = jax.ShapeDtypeStruct((rows, bond), jnp.float32)
        scratch = [pltpu.VMEM((rows * states, bond), jnp.float32), pltpu.SemaphoreType.DMA((2 + rows // min(rows, 16),))]
        if first:
            scratch.append(pltpu.SMEM(block_dims.shape, block_dims.dtype))
        return pl.pallas_call(
            functools.partial(finish_kernel, first, rows, states, bond),
            out_shape=(out, keep) if first else out,
            in_specs=[ANY] + [VMEM] * (len(operands) - 1),
            out_specs=(ANY, VMEM) if first else ANY,
            scratch_shapes=scratch,
            input_output_aliases={} if first else {0: 0},
            compiler_params=PARAMS,
            cost_estimate=LIGHT,
            name="finish_first" if first else "finish_second",
        )(*operands)

    first_parts[1], *operands = lax.optimization_barrier((first_parts[1], *operands))
    call = Call("second_mine", False, mine, **far)
    (second_mine,) = apply_terms(call, sizes, tables, operands)
    second_mine, first_mine = lax.optimization_barrier((second_mine, first_mine))
    out, keep = finish(True, dims, first_mine, *first_parts)
    out = finish(False, out, keep, second_mine, *second_parts)
    return out.reshape(sectors, rows, states, bond)


def solution(mesh):
    placed = (
        P("blk", None, None, None),
        P("blk", None),
        P(None, "blk"),
        P(),
        P("mpo", "blk", None, None),
        P("mpo", "blk", None, None),
        P(),
        P(),
    )
    return jax.shard_map(
        body, mesh=mesh, in_specs=placed, out_specs=P("blk", "mpo", None, None), check_vma=False
    )
```

```python
import functools

import jax
import jax.numpy as jnp
from jax import lax
from jax.experimental import pallas as pl
from jax.experimental.pallas import tpu as pltpu
from jax.sharding import PartitionSpec as P

VMEM = pl.BlockSpec(memory_space=pltpu.VMEM)
ANY = pl.BlockSpec(memory_space=pl.ANY)
PARAMS = pltpu.CompilerParams(vmem_limit_bytes=24 * 1024 * 1024)
LIGHT = pl.CostEstimate(flops=1, bytes_accessed=1, transcendentals=0)


def split(x):
    high = x.astype(jnp.bfloat16)
    low = (x - high.astype(jnp.float32)).astype(jnp.bfloat16)
    return high, low


def weighted(scales, values):
    total = scales[0] * values[0]
    for scale, value in zip(scales[1:], values[1:]):
        total = total + scale * value
    return total


def local_sector(blk, first):
    odd = lax.rem(blk, 2)
    return 1 - odd if first else odd


def partner_of(z):
    return z + 1 - 2 * lax.rem(z, 2)


def row_start(z, parity, r, groups, rows):
    dest = lax.rem(lax.div(z, 2) + r, groups) * 2 + parity
    return pl.multiple_of(dest * rows, rows)


def env_copies(first, sides, groups, rows, left_ref, right_ref, env_ref, sem, skip=0):
    z = lax.axis_index("mpo")
    some = slice(skip, skip + env_ref.shape[0])
    sector = local_sector(lax.axis_index("blk"), first)
    bond = right_ref.shape[-1]
    copies, at = [], 0
    for own in sides:
        for r in range(groups):
            start = row_start(z, lax.rem(z if own else partner_of(z), 2), r, groups, rows)
            source = left_ref.at[some, sector, pl.ds(start, rows), :]
            copies.append(pltpu.make_async_copy(source, env_ref.at[:, at : at + rows, :], sem.at[len(copies)]))
            at += rows
    source = right_ref.at[some, sector]
    copies.append(pltpu.make_async_copy(source, env_ref.at[:, at : at + bond, :], sem.at[len(copies)]))
    return copies


def front_kernel(groups, rows, states, dims_ref, theta_ref, left_ref, right_ref, *refs):
    outer_ref, inner_ref, early_ref, last_ref, dims, held, sem, early_sem, last_sem = refs
    blk = lax.axis_index("blk")
    fetches = [pltpu.make_async_copy(dims_ref, dims, sem.at[2])]
    for i, first in enumerate((False, True)):
        fetches.append(pltpu.make_async_copy(theta_ref.at[local_sector(blk, first)], held.at[i], sem.at[i]))
    copies = env_copies(False, (False,), groups, rows, left_ref, right_ref, early_ref, early_sem)
    copies += env_copies(False, (False,), groups, rows, left_ref, right_ref, last_ref, last_sem, early_ref.shape[0])
    for copy in fetches + copies:
        copy.start()
    step = 256
    fetches[0].wait()
    for i, (first, out_ref) in enumerate(((False, outer_ref), (True, inner_ref))):
        sector = local_sector(blk, first)
        fetches[i + 1].wait()

        def part(j, carry, i=i, out_ref=out_ref, sector=sector):
            start = pl.multiple_of(j * step, step)
            row = lax.broadcasted_iota(jnp.int32, (step, held.shape[2]), 0) + start
            col = lax.broadcasted_iota(jnp.int32, (step, held.shape[2]), 1)
            keep = (row < dims[sector, 0] * states) & (col < dims[sector, 1])
            out_ref[pl.ds(start, step), :] = jnp.where(keep, held[i, pl.ds(start, step), :], 0.0)
            return carry

        lax.fori_loop(0, held.shape[1] // step, part, 0)
    for copy in copies:
        copy.wait()


class Call:
    def __init__(self, name, first, cuts, slots=(), own=(), packets=(), added=False, near=None, whole=()):
        self.name, self.first, self.cuts, self.slots = name, first, cuts, slots
        self.own, self.packets, self.added, self.near = own, packets, added, near
        self.leads = 0 in slots
        self.far = slots == (2,)
        self.whole = whole
        self.kept = not slots or bool(whole)


def apply_kernel(call, groups, rows, bond, site, terms, *refs):
    refs = list(refs)
    take = lambda count: [refs.pop(0) for _ in range(count)]
    table_refs = take(4)
    blocks = take(len(call.slots))
    kept = source = take(1)[0] if call.kept else None
    left_ref, right_ref = take(2) if call.own else (None, None)
    packets = take(len(call.packets))
    before_ref = take(1)[0] if call.added else None
    outs = take(len(call.cuts))
    if call.slots:
        source = take(1)[0]
    moved, mixed, charge_ref, allowed_ref, one_ref, two_ref, sem = take(7)
    states = site * site
    z = lax.axis_index("mpo")
    sector = local_sector(lax.axis_index("blk"), call.first)
    low, high = call.cuts[0][0], call.cuts[-1][1]
    tall = high - low
    block = min(rows, 16)
    joined = 16 // block

    tables = (charge_ref, allowed_ref, one_ref, two_ref)
    copies = [pltpu.make_async_copy(a, b, sem.at[i]) for i, (a, b) in enumerate(zip(table_refs, tables))]
    sides = [(packet, partner_of(z) * terms + skip, call.near) for packet, skip in zip(packets, call.packets)]
    sides += [(packets[i], partner_of(z) * terms + call.packets[i], True) for i in call.whole]
    if call.own:
        env, env_sem = take(2)
        copies += env_copies(call.first, call.own, groups, rows, left_ref, right_ref, env, env_sem)
        sides.append((env, z * terms, call.near))
    late = copies[len(tables) :]
    copies = copies[: len(tables)]
    for copy in copies + late:
        copy.start()

    for i, ref in enumerate(blocks):

        def part(s, carry, i=i, ref=ref):
            for u in range(0, site, 2):
                pieces = [split(ref[pl.ds(s * site + u + k, bond, stride=states), :]) for k in range(2)]
                cut = pl.ds(pl.multiple_of((s * site + u) * bond, bond), 2 * bond)
                source[i, 0:bond, cut] = jnp.concatenate([pieces[0][0], pieces[1][0]], axis=1)
                source[i, bond : 2 * bond, cut] = jnp.concatenate([pieces[0][1], pieces[1][1]], axis=1)
            return carry

        lax.fori_loop(0, site, part, 0, unroll=2)

    at = low * states
    for out in outs:
        out[...] = before_ref[at : at + out.shape[0], :] if call.added else jnp.zeros_like(out)
        at += out.shape[0]
    for copy in copies:
        copy.wait()

    def add_term(env, w, term, source, slot):
        left = env[w, low:high, :]
        left_rest = left - left.astype(jnp.bfloat16).astype(jnp.float32)
        stacked = jnp.concatenate([left, left_rest], axis=0).astype(jnp.bfloat16)
        rows_in = jnp.concatenate([stacked, stacked], axis=1)
        for s in range(site):
            cut = slice(s * site * bond, (s + 1) * site * bond)
            moved[:, cut] = jnp.dot(rows_in, source[slot, :, cut], preferred_element_type=jnp.float32)
        one = [[one_ref[i, j, term] for j in range(site)] for i in range(site)]
        two = [[two_ref[i, j, term] for j in range(site)] for i in range(site)]
        right = env[w, env.shape[1] - bond :, :]
        folded = jnp.concatenate(split(jnp.transpose(right)), axis=1)
        weights = jnp.concatenate([folded, folded], axis=0)
        for start in range(0, tall, block):
            half = []
            for s in range(site):
                cols = []
                for u in range(site):
                    cut = slice((s * site + u) * bond, (s * site + u + 1) * bond)
                    cols.append(moved[start : start + block, cut] + moved[tall + start : tall + start + block, cut])
                half.append([weighted(two[v], cols) for v in range(site)])
            values = [weighted(one[t], [half[s][v] for s in range(site)]) for t in range(site) for v in range(site)]
            base, size = start * states, block * states
            for p in range(0, states, joined):
                upper, lower = split(jnp.concatenate(values[p : p + joined], axis=0) if joined > 1 else values[p])
                here = base + p * block
                mixed[here : here + joined * block, 0:bond] = upper
                mixed[here : here + joined * block, bond : 2 * bond] = lower
            got = jnp.dot(mixed[base : base + size, :], weights, preferred_element_type=jnp.float32)
            got = got[:, :bond] + got[:, bond:]
            for (first_row, last_row), out in zip(call.cuts, outs):
                if first_row <= low + start < last_row:
                    at = (low + start - first_row) * states
                    out[at : at + size, :] += got

    for n, (env, first_term, near) in enumerate(sides):
        if n == len(sides) - 1:
            for copy in late:
                copy.wait()

        def one_term(w, carry, env=env, first_term=first_term, near=near):
            term = first_term + w
            charge = charge_ref[term]
            shifted = sector - charge
            inside = (shifted >= 0) & (shifted <= 1)
            wanted = allowed_ref[sector, term] != 0
            if near is not None:
                wanted = wanted & (inside if near else jnp.logical_not(inside))
            chosen = source
            if call.far and not near:
                slot = 0
            else:
                chosen = kept if call.kept else source
                slot = jnp.where(inside, jnp.where(charge == 0, 0 if call.first else 1, 1 if call.first else 0), 2)

            @pl.when(wanted)
            def _():
                add_term(env, w, term, chosen, slot)

            return carry

        lax.fori_loop(0, env.shape[0], one_term, 0)


def apply_terms(call, sizes, tables, operands):
    groups, rows, bond, site, terms = sizes
    states = site * site
    height = groups * rows
    tall = call.cuts[-1][1] - call.cuts[0][0]
    scratch = [
        pltpu.VMEM((2 * tall, states * bond), jnp.float32),
        pltpu.VMEM((states * tall, 2 * bond), jnp.bfloat16),
    ]
    scratch += [pltpu.SMEM(x.shape, x.dtype) for x in tables]
    scratch.append(pltpu.SemaphoreType.DMA((len(tables),)))
    places = [ANY] * 4 + [VMEM] * (len(call.slots) + call.kept)
    if call.own:
        places += [ANY, ANY]
        count = len(call.own)
        scratch.append(pltpu.VMEM((terms, count * height + bond, bond), jnp.float32))
        scratch.append(pltpu.SemaphoreType.DMA((count * groups + 1,)))
    places += [VMEM] * (len(call.packets) + call.added)
    out = [jax.ShapeDtypeStruct(((b - a) * states, bond), jnp.float32) for a, b in call.cuts]
    shape = (len(call.slots), 2 * bond, states * bond)
    if call.leads:
        out.append(jax.ShapeDtypeStruct(shape, jnp.bfloat16))
    elif call.slots:
        scratch.insert(0, pltpu.VMEM(shape, jnp.bfloat16))
    return pl.pallas_call(
        functools.partial(apply_kernel, call, *sizes),
        out_shape=tuple(out),
        in_specs=places,
        out_specs=(VMEM,) * len(out),
        scratch_shapes=scratch,
        compiler_params=PARAMS,
        cost_estimate=LIGHT,
        name=call.name,
    )(*tables, *operands)


def join_kernel(mine_ref, got_ref, out_ref):
    out_ref[...] = mine_ref[...] + got_ref[...]


def finish_kernel(first, rows, states, bond, *refs):
    if first:
        dims_ref, *parts, out_ref, keep_ref, held, sem, dims = refs
        copy = pltpu.make_async_copy(dims_ref, dims, sem.at[1])
        copy.start()
        copy.wait()
    else:
        _, keep_ref, *parts, out_ref, held, sem = refs
    blk = lax.axis_index("blk")
    sector = local_sector(blk, first)
    block = min(rows, 16)

    def mask(sector, start):
        row = lax.broadcasted_iota(jnp.int32, (block, bond), 0) + (lax.axis_index("mpo") * rows + start)
        col = lax.broadcasted_iota(jnp.int32, (block, bond), 1)
        return ((row < dims[sector, 0]) & (col < dims[sector, 1])).astype(jnp.float32)

    copies = []
    for start in range(0, rows, block):
        if first:
            keep = mask(sector, start)
            keep_ref[start : start + block, :] = mask(local_sector(blk, False), start)
        else:
            keep = keep_ref[start : start + block, :]
        for p in range(states):
            at = start * states + p * block
            value = parts[0][at : at + block, :]
            for other in parts[1:]:
                value = value + other[at : at + block, :]
            held[pl.ds(start * states + p, block, stride=states), :] = value * keep
        some = pl.ds(start * states, block * states)
        copies.append(pltpu.make_async_copy(held.at[some, :], out_ref.at[sector, some, :], sem.at[2 + len(copies)]))
        copies[-1].start()
    for copy in copies:
        copy.wait()


def body(theta, block_dims, pair_mask, term_charge, left_env, right_env, site_one, site_two):
    sectors, bond, states, _ = theta.shape
    blk_count, group_count = lax.axis_size("blk"), lax.axis_size("mpo")
    terms = left_env.shape[0]
    rows = bond // group_count
    groups = group_count // 2
    height = groups * rows
    swap = [(i, i ^ 1) for i in range(group_count)]
    flat = pltpu.with_memory_space_constraint(theta.reshape(sectors, bond * states, bond), pltpu.HBM)
    left_env = pltpu.with_memory_space_constraint(left_env, pltpu.HBM)
    right_env = pltpu.with_memory_space_constraint(right_env, pltpu.HBM)
    dims = pltpu.with_memory_space_constraint(block_dims, pltpu.HBM)

    sector_block = jax.ShapeDtypeStruct((bond * states, bond), jnp.float32)
    last = max(terms // 3, 1)
    early = terms - last
    packets = [jax.ShapeDtypeStruct((count, height + bond, bond), jnp.float32) for count in (early, last)]

    outer, inner, early_packed, last_packed = pl.pallas_call(
        functools.partial(front_kernel, groups, rows, states),
        out_shape=(sector_block, sector_block, *packets),
        in_specs=[ANY] * 4,
        out_specs=(VMEM,) * 4,
        scratch_shapes=[
            pltpu.SMEM(block_dims.shape, block_dims.dtype),
            pltpu.VMEM((2, bond * states, bond), jnp.float32),
            pltpu.SemaphoreType.DMA((3,)),
            pltpu.SemaphoreType.DMA((groups + 1,)),
            pltpu.SemaphoreType.DMA((groups + 1,)),
        ],
        compiler_params=PARAMS,
        cost_estimate=LIGHT,
        name="front",
    )(dims, flat, left_env, right_env)
    tables = (term_charge, pair_mask.T, site_one.transpose(1, 2, 0), site_two.transpose(1, 2, 0))
    pairs = blk_count // 2
    crossing = [(2 * i + 1, 2 * i + 2) for i in range(pairs - 1)]
    halo_second = lax.ppermute(outer, "blk", crossing + [(b, a) for a, b in crossing])
    halo_first = lax.ppermute(inner, "blk", [(i, i ^ 1) for i in range(2 * pairs)])
    early_env = lax.ppermute(early_packed, "mpo", swap)

    sizes = (groups, rows, bond, site_one.shape[-1], terms)
    every, mine, rest = [(0, height)], [(0, rows)], [(rows, height)]
    theirs = [(height, height + rows), (height + rows, 2 * height)]
    envs = (left_env, right_env)

    call = Call("first_own", True, mine + rest + theirs, slots=(0, 1, 2), own=(True, False))
    operands = (inner, outer, halo_first, *envs)
    first_mine, first_rest, mine_away, rest_away, source = apply_terms(call, sizes, tables, operands)
    rest_away, last_packed = lax.optimization_barrier((rest_away, last_packed))
    rest_got = lax.ppermute(rest_away, "mpo", swap)
    last_env = lax.ppermute(last_packed, "mpo", swap)
    call = Call("second_near", False, every, own=(True,), packets=(0,), near=True)
    (before,) = apply_terms(call, sizes, tables, (source, *envs, early_env))
    rest_got, before = lax.optimization_barrier((rest_got, before))
    first_rest = pl.pallas_call(
        join_kernel,
        out_shape=jax.ShapeDtypeStruct(first_rest.shape, first_rest.dtype),
        in_specs=[VMEM] * 2,
        out_specs=VMEM,
        compiler_params=PARAMS,
        cost_estimate=LIGHT,
        name="join",
    )(first_rest, rest_got)
    first_rest, before = lax.optimization_barrier((first_rest, before))
    operands = (halo_second, source, *envs, early_env, last_env, before)
    far = dict(slots=(2,), own=(True,), packets=(0, early), added=True, near=False, whole=(1,))
    call = Call("second_rest", False, rest, **far)
    (second_rest,) = apply_terms(call, sizes, tables, operands)
    second_rest, mine_away = lax.optimization_barrier((second_rest, mine_away))
    mine_got = lax.ppermute(mine_away, "mpo", swap)

    first_parts, second_parts = [mine_got], []
    cut = rows * states
    for r in range(1, groups):
        route = [(i, ((i // 2 + r) % groups) * 2 + i % 2) for i in range(group_count)]
        first_parts.append(lax.ppermute(first_rest[(r - 1) * cut : r * cut], "mpo", route))
        second_parts.append(lax.ppermute(second_rest[(r - 1) * cut : r * cut], "mpo", route))

    def finish(first, *operands):
        out = jax.ShapeDtypeStruct((sectors, rows * states, bond), jnp.float32)
        keep = jax.ShapeDtypeStruct((rows, bond), jnp.float32)
        scratch = [pltpu.VMEM((rows * states, bond), jnp.float32), pltpu.SemaphoreType.DMA((2 + rows // min(rows, 16),))]
        if first:
            scratch.append(pltpu.SMEM(block_dims.shape, block_dims.dtype))
        return pl.pallas_call(
            functools.partial(finish_kernel, first, rows, states, bond),
            out_shape=(out, keep) if first else out,
            in_specs=[ANY] + [VMEM] * (len(operands) - 1),
            out_specs=(ANY, VMEM) if first else ANY,
            scratch_shapes=scratch,
            input_output_aliases={} if first else {0: 0},
            compiler_params=PARAMS,
            cost_estimate=LIGHT,
            name="finish_first" if first else "finish_second",
        )(*operands)

    first_parts[1], *operands = lax.optimization_barrier((first_parts[1], *operands))
    call = Call("second_mine", False, mine, **far)
    (second_mine,) = apply_terms(call, sizes, tables, operands)
    second_mine, first_mine = lax.optimization_barrier((second_mine, first_mine))
    out, keep = finish(True, dims, first_mine, *first_parts)
    out = finish(False, out, keep, second_mine, *second_parts)
    return out.reshape(sectors, rows, states, bond)


def solution(mesh):
    placed = (
        P("blk", None, None, None),
        P("blk", None),
        P(None, "blk"),
        P(),
        P("mpo", "blk", None, None),
        P("mpo", "blk", None, None),
        P(),
        P(),
    )
    return jax.shard_map(
        body, mesh=mesh, in_specs=placed, out_specs=P("blk", "mpo", None, None), check_vma=False
    )
```
